256 devices in a mesh: dp: 64 (over z_lo, x, y, core), tensor: 4 (over z_hi).
Axes of the slice: x: 4, y: 4, z: 8 (z_hi: 4, z_lo: 2; z = z_hi * 2 + z_lo), core: 2. Of those that a mesh axis runs over, the one named last changes fastest.
Arguments:
- activations: bfloat16 [2, 2, 32768, 5120], P(None, None, ('dp', 'tensor')), may hold values from -60 to 60
- grad_qkv: bfloat16 [2, 15360, 5120], P(None, 'dp', 'tensor'), may hold values from -60 to 60
- grad_up: bfloat16 [2, 20480, 5120], P(None, 'dp', 'tensor'), may hold values from -60 to 60
- newton_steps: int32 [2, 2, 8], replicated, may hold values from 2 to 4, as said below
Outputs:
- precond_qkv: bfloat16 [2, 15360, 5120], P(None, 'dp', 'tensor')
- precond_up: bfloat16 [2, 20480, 5120], P(None, 'dp', 'tensor')
The draws below stay inside these ranges and needn't reach their ends.
Inputs may be any that keep to these rules, and one draw needn't show every extreme that they name: `newton_steps`: one count for each diagonal block; some block takes all 4 iterations.
All inputs are finite; a program needn't handle non-finite values.
Results may differ from the reference program's by a relative error of at most 0.0051.
Values may be sent and summed in bfloat16 or wider, within the bound.
No kernel may reach another device: no remote copies, remote signals or barrier semaphores. Data moves between devices by JAX's collectives and lax.ppermute only.
A program may use at most 128 MiB of HBM per device.

```python
import jax
import jax.numpy as jnp
from jax import lax

D = 5120
L = 2
ITERS = 4
TOKENS = 32768
BLOCK = 640


def draw_activations(key, part):
    key = jax.random.fold_in(key, 11)
    keys = jax.random.split(key, 6)
    shape = (L, 2, TOKENS, D)
    noise = jnp.clip(jax.random.normal(keys[0], shape, jnp.float32), -5.0, 5.0)
    common = 0.1
    spread = 0.5
    shift_key, sign_key, weight_key = jax.random.split(keys[5], 3)
    shifts = jax.random.randint(shift_key, (8,), 1, BLOCK)
    signs = jnp.where(jax.random.bernoulli(sign_key, 0.5, (8,)), 1.0, -1.0)
    weights = signs * jax.random.uniform(weight_key, (8,), jnp.float32, 0.25, 0.45)
    mixed = noise
    for shift_index in range(8):
        mixed = mixed + weights[shift_index] * jnp.roll(noise, shifts[shift_index], axis=3)
    latent = jnp.clip(jax.random.normal(keys[1], (L, 2, TOKENS, 4), jnp.float32), -4.0, 4.0)
    loadings = jnp.clip(jax.random.normal(keys[2], (L, 2, 4, D), jnp.float32), -4.0, 4.0)
    for factor_index in range(4):
        mixed = mixed + common * latent[:, :, :, factor_index:factor_index + 1] * loadings[:, :, None, factor_index, :]
    column_scale = jnp.exp(jax.random.uniform(keys[3], (L, 2, 1, D), jnp.float32, 0.0, 1.19))
    position = jnp.arange(TOKENS, dtype=jnp.float32) / TOKENS
    row_scale = jnp.exp(1.0986 * position[None, None, :, None] + jax.random.uniform(keys[4], (L, 2, TOKENS, 1), jnp.float32, 0.0, spread))
    return jnp.clip(mixed * column_scale * row_scale, -60.0, 60.0).astype(jnp.bfloat16)


def draw_newton_steps(key, part):
    key = jax.random.fold_in(key, 23)
    count_key, place_key = jax.random.split(key)
    shape = (L, 2, D // BLOCK)
    counts = jax.random.randint(count_key, shape, ITERS // 2, ITERS + 1)
    chosen = jax.random.randint(place_key, (), 0, L * 2 * (D // BLOCK))
    flattened = counts.reshape(-1)
    flattened = jnp.where(jnp.arange(flattened.shape[0]) == chosen, ITERS, flattened)
    return flattened.reshape(shape).astype(jnp.int32)


def levels(key, shape, shards, low, top_value):
    factor_of = 1.0
    for dim, shards_of in shards:
        heights = jax.random.uniform(jax.random.fold_in(jax.random.fold_in(key, 6), dim), (shards_of,), jnp.float32, low / len(shards), top_value / len(shards))
        factor_of = factor_of * jnp.repeat(jnp.exp(heights), shape[dim] // shards_of).reshape((-1,) + (1,) * (len(shape) - 1 - dim))
    return factor_of


def scatter_about(own_key, shape, width, limit, cuts=(), held_as=jnp.bfloat16):
    entries = width * jax.random.normal(own_key, shape, jnp.float32)
    if cuts:
        entries = entries * levels(own_key, shape, cuts, -0.22, 0.18)
    return jnp.clip(entries, -limit, limit).astype(held_as)


def setup_inputs(seed: int = 0) -> dict:
    splits = jax.random.split(jax.random.key(seed), 5)
    return {
        "activations": draw_activations(jax.random.fold_in(splits[4], 71), 0),
        "grad_qkv": scatter_about(splits[1], (L, 3 * D, D), 10.0, 60.0, ((1, 64), (2, 4))),
        "grad_up": scatter_about(splits[2], (L, 4 * D, D), 10.0, 60.0, ((1, 64), (2, 4))),
        "newton_steps": draw_newton_steps(jax.random.fold_in(splits[4], 71), 0),
    }


damping = 0.05

def newton_inverse(factor, step_count):
    eye_block = jnp.eye(factor.shape[0], dtype=jnp.float32)
    norm_scale = jnp.sqrt(jnp.sum(factor * factor))
    inverse = eye_block / norm_scale
    mixed = factor / norm_scale
    for turn_index in range(ITERS):
        reflect = 2.0 * eye_block - mixed
        new_inverse = jnp.dot(inverse, reflect, precision=lax.Precision.HIGHEST)
        new_mixed = jnp.dot(mixed, reflect, precision=lax.Precision.HIGHEST)
        active_turn = turn_index < step_count
        inverse = jnp.where(active_turn, new_inverse, inverse)
        mixed = jnp.where(active_turn, new_mixed, mixed)
    return inverse.astype(jnp.bfloat16)

def reference(activations, grad_qkv, grad_up, newton_steps):
    block_count = D // BLOCK
    eye_block = jnp.eye(BLOCK, dtype=jnp.float32)
    results = []
    for kind_index, gradient in ((0, grad_qkv), (1, grad_up)):
        layer_outs = []
        for layer_index in range(L):
            inputs = activations[layer_index, kind_index]
            pieces = []
            for block_index in range(block_count):
                columns = inputs[:, block_index * BLOCK:(block_index + 1) * BLOCK]
                factor = jnp.dot(columns.T, columns, preferred_element_type=jnp.float32) / TOKENS + damping * eye_block
                inverse = newton_inverse(factor, newton_steps[layer_index, kind_index, block_index])
                grad_piece = gradient[layer_index][:, block_index * BLOCK:(block_index + 1) * BLOCK]
                pieces.append(jnp.dot(grad_piece, inverse, preferred_element_type=jnp.float32).astype(jnp.bfloat16))
            layer_outs.append(jnp.concatenate(pieces, 1))
        results.append(jnp.stack(layer_outs))
    return (results[0], results[1])
```

```python
import functools

import jax
import jax.numpy as jnp
from jax import lax
from jax.experimental import pallas as pl
from jax.experimental.pallas import tpu as pltpu
from jax.sharding import PartitionSpec as P

DAMPING = 0.05
BLOCK = 640
TILE = 128
PACK = 384
PANELS = ((0, 0), (128, 0), (256, 0), (256, 384), (128, 512))
RING = 4
CHUNK = PACK // RING
PIECE = CHUNK // 2
VMEM_BYTES = 48 * 1024 * 1024
AXES = ("dp", "tensor")
PARAMS = pltpu.CompilerParams(vmem_limit_bytes=VMEM_BYTES)
SMEM = pl.BlockSpec(memory_space=pltpu.SMEM)
VMEM = pl.BlockSpec(memory_space=pltpu.VMEM)
ANY = pl.BlockSpec(memory_space=pl.ANY)


def move(array, target):
    pairs = []
    for source in range(256):
        dp, t = source // 4, source % 4
        zl, x, y, c = dp // 32, dp // 8 % 4, dp // 2 % 4, dp % 2
        zl2, x2, y2, c2, t2 = target(zl, x, y, c, t)
        pairs.append((source, (((zl2 * 4 + x2) * 4 + y2) * 2 + c2) * 4 + t2))
    return lax.ppermute(array, AXES, pairs)


def by_layer(layer, shift, flip_core=0):
    def target(zl, x, y, c, t):
        if layer == 0:
            return zl, (x + shift) % 4, y, c ^ flip_core, t
        return zl, x, (y + shift) % 4, c ^ flip_core, t

    return target


def round_z(shift):
    def target(zl, x, y, c, t):
        z = (2 * t + zl + shift) % 8
        return z % 2, x, y, c, z // 2

    return target


def own_layer(c, t):
    return 0 if t // 2 == c else 1


def in_group(shift, flip):
    def target(zl, x, y, c, t):
        if own_layer(c, t) == 0:
            return zl ^ flip, x, (y + shift) % 4, c, t
        return zl ^ flip, (x + shift) % 4, y, c, t

    return target


def across_groups(shift):
    def target(zl, x, y, c, t):
        if own_layer(c, t) == 0:
            return zl, (x + shift) % 4, y, c, t
        return zl, x, (y + shift) % 4, c, t

    return target


def other_core(zl, x, y, c, t):
    return zl, x, y, 1 - c, t


def ds(start, size, unit):
    return pl.ds(pl.multiple_of(start, unit), size)


def pack_kernel(info, act, *refs):
    outs, sem = refs[:-1], refs[-1]
    copies = []
    number = 0
    for layer in range(2):
        place = info[layer]
        for flip in range(2):
            half = info[3] ^ (flip ^ layer)
            for shift in range(RING):
                there = lax.rem(place + shift, RING)
                kind, first = there // 2, 4 * half + lax.rem(there, 2)
                for k in range(2):
                    copies.append(
                        pltpu.make_async_copy(
                            act.at[layer, kind, :, ds((first + 2 * k) * BLOCK, BLOCK, TILE)],
                            outs[number].at[k],
                            sem.at[2 * number + k],
                        )
                    )
                    copies[-1].start()
                number += 1
    for copy in copies:
        copy.wait()


def pack_panels(read, write):
    for i, (row, col) in enumerate(PANELS):
        write(row, col, read(i))


def gram_kernel(info, *refs):
    ins, outs = refs[:16], refs[16:24]
    tokens, tri, sem = refs[24:]
    rows = ins[0].shape[1]
    copies = []
    for layer in range(2):
        for part in range(8):
            number = 8 * layer + part
            copies.append(
                pltpu.make_async_copy(
                    ins[number],
                    tokens.at[layer, :, pl.ds(part * rows, rows), :],
                    sem.at[number],
                )
            )
            copies[-1].start()
    for layer in range(2):
        for copy in copies[8 * layer : 8 * layer + 8]:
            copy.wait()
        place = info[1 - layer]
        for k in range(2):

            def product(low, high):
                return lax.dot_general(
                    tokens[layer, k, :, low:high],
                    tokens[layer, k, :, low:],
                    (((0,), (0,)), ((), ())),
                    preferred_element_type=jnp.float32,
                )

            top = product(0, 256)
            tri[0:128, :] = top[0:128]
            tri[128:256, 0:512] = top[128:256, 128:]
            middle = product(256, 512)
            tri[256:384, 0:384] = middle[0:128]
            tri[256:384, 384:640] = middle[128:256, 128:]
            tri[128:256, 512:640] = product(512, 640)
            for shift in range(RING):
                there = lax.rem(place + shift, RING)
                out = outs[RING * layer + shift]
                out[k] = tri[ds(there * CHUNK, CHUNK, 32), :].astype(out.dtype)


def slab_kernel(info, *refs):
    ins, outs, total = refs[:8], refs[8:16], refs[16]
    for layer in range(2):
        for k in range(2):
            parts = ins[RING * layer : RING * layer + RING]
            value = parts[0][k]
            for part in parts[1:]:
                value = value + part[k].astype(jnp.float32)
            total[2 * (info[3] ^ layer) + k] = value
    z = 2 * info[4] + info[2]
    for shift in range(8):
        there = lax.rem(z + shift, 8)
        out = outs[shift]
        out[...] = total[there // 2, ds(lax.rem(there, 2) * PIECE, PIECE, 16), :].astype(out.dtype)


def newton_kernel(tokens_all, info, *refs):
    ins, out = refs[:8], refs[8]
    tri, mixed, gap, mixed_half = refs[9:]
    place = jnp.where(info[5] == 0, info[1], info[0])
    for number in range(8):
        shift, flip = number // 2, number % 2
        source = lax.rem(place + (RING - shift), RING)
        start = source * CHUNK + (info[2] ^ flip) * PIECE
        tri[ds(start, PIECE, 16), :] = ins[number][...].astype(jnp.float32)
    for i, (row, col) in enumerate(PANELS):
        low = TILE * i
        panel = tri[row : row + TILE, col : col + BLOCK - low]
        mixed[low : low + TILE, low:] = panel
        if i < 4:
            mixed[low + TILE :, low : low + TILE] = panel[:, TILE:].T
    eye = (
        lax.broadcasted_iota(jnp.int32, (BLOCK, BLOCK), 0)
        == lax.broadcasted_iota(jnp.int32, (BLOCK, BLOCK), 1)
    ).astype(jnp.float32)
    factor = mixed[...] * (1.0 / tokens_all) + DAMPING * eye
    norm_scale = jnp.sqrt(jnp.sum(factor * factor))
    mixed[...] = factor / norm_scale
    steps = info[7]

    def dot(a, b):
        return jnp.dot(a.astype(jnp.bfloat16), b, preferred_element_type=jnp.float32)

    gap[...] = mixed[...]
    power = 2.0
    for turn in range(1, 4):
        half = mixed[...].astype(jnp.bfloat16)
        mixed_half[...] = half
        mixed[...] = 2.0 * mixed[...] - dot(half, mixed_half[...])
        mixed_half[...] = mixed[...].astype(jnp.bfloat16)
        new_gap = 2.0 * gap[...] + power * mixed[...] - dot(gap[...], mixed_half[...])
        gap[...] = jnp.where(turn < steps, new_gap, gap[...])
        power = 2.0 * power
    reach = jnp.where(steps <= 1, 2.0, jnp.where(steps == 2, 4.0, jnp.where(steps == 3, 8.0, 16.0)))
    scale = 1.0 / norm_scale
    for i, (row, col) in enumerate(PANELS):
        low = TILE * i
        value = (reach * eye[low : low + TILE, low:] - gap[low : low + TILE, low:]) * scale
        out[row : row + TILE, col : col + BLOCK - low] = value.astype(jnp.bfloat16)


def apply_kernel(info, grad_qkv, grad_up, *refs):
    ins, outs = refs[:8], refs[8:10]
    packed, whole, sem = refs[10:]
    grads = (grad_qkv, grad_up)
    copies = []
    for number in range(8):
        mine, shift = number // RING, number % RING
        layer = info[5] ^ mine
        place = jnp.where(layer == 0, info[0], info[1])
        source = lax.rem(place + (RING - shift), RING)
        copies.append(
            pltpu.make_async_copy(ins[number], packed.at[RING * layer + source], sem.at[number])
        )
        copies[-1].start()
    for copy in copies:
        copy.wait()
    for layer in range(2):
        for kind in range(2):
            for j in range(2):
                block = RING * layer + 2 * kind + j
                for i, (row, col) in enumerate(PANELS):
                    low = TILE * i
                    panel = packed[block, row : row + TILE, col : col + BLOCK - low]
                    whole[low : low + TILE, low:] = panel
                    if i < 4:
                        whole[low + TILE :, low : low + TILE] = panel[:, TILE:].T
                columns = slice(j * BLOCK, (j + 1) * BLOCK)
                outs[kind][layer, :, columns] = jnp.dot(
                    grads[kind][layer, :, columns],
                    whole[...],
                    preferred_element_type=jnp.float32,
                ).astype(jnp.bfloat16)


def local(activations, grad_qkv, grad_up, newton_steps):
    dp, t = lax.axis_index("dp"), lax.axis_index("tensor")
    zl, x, y, c = dp // 32, dp // 8 % 4, dp // 2 % 4, dp % 2
    layer = jnp.where(t // 2 == c, 0, 1)
    place = jnp.where(layer == 0, x, y)
    steps = newton_steps.reshape(-1)[16 * layer + 8 * (place // 2) + 2 * t + place % 2]
    info = jnp.stack([x, y, zl, c, t, layer, place, steps]).astype(jnp.int32)
    rows = activations.shape[2]
    tokens_all = rows * 256
    half = jnp.bfloat16

    def shape(dims, dtype=half):
        return jax.ShapeDtypeStruct(dims, dtype)

    pieces = pl.pallas_call(
        pack_kernel,
        out_shape=[shape((2, rows, BLOCK))] * 16,
        in_specs=[SMEM, ANY],
        out_specs=[ANY] * 16,
        scratch_shapes=[pltpu.SemaphoreType.DMA((32,))],
        compiler_params=PARAMS,
        name="pack",
    )(info, activations)
    here = []
    for number, piece in enumerate(pieces):
        of_layer, flip, shift = number // 8, number // 4 % 2, number % 4
        if flip or shift:
            piece = move(piece, by_layer(of_layer, shift, flip))
        here.append(piece)

    chunks = pl.pallas_call(
        gram_kernel,
        out_shape=[
            shape((2, CHUNK, BLOCK), half if shift else jnp.float32)
            for _ in range(2)
            for shift in range(RING)
        ],
        in_specs=[SMEM] + [ANY] * 16,
        out_specs=[VMEM] * 8,
        scratch_shapes=[
            pltpu.VMEM((2, 2, 8 * rows, BLOCK), half),
            pltpu.VMEM((PACK, BLOCK), jnp.float32),
            pltpu.SemaphoreType.DMA((16,)),
        ],
        compiler_params=PARAMS,
        name="gram",
    )(info, *here)
    chunks = [
        move(chunk, by_layer(1 - number // RING, number % RING)) if number % RING else chunk
        for number, chunk in enumerate(chunks)
    ]

    slabs = pl.pallas_call(
        slab_kernel,
        out_shape=[shape((PIECE, BLOCK), half if shift else jnp.float32) for shift in range(8)],
        in_specs=[SMEM] + [VMEM] * 8,
        out_specs=[VMEM] * 8,
        scratch_shapes=[pltpu.VMEM((4, CHUNK, BLOCK), jnp.float32)],
        compiler_params=PARAMS,
        name="slab",
    )(info, *chunks)
    total = slabs[0]
    for moved in [move(slabs[shift], round_z(shift)) for shift in range(1, 8)]:
        total = total + moved.astype(jnp.float32)
    total = total.astype(half)

    members = [total] + [move(total, in_group(n // 2, n % 2)) for n in range(1, 8)]
    inverse = pl.pallas_call(
        functools.partial(newton_kernel, tokens_all),
        out_shape=shape((PACK, BLOCK)),
        in_specs=[SMEM] + [VMEM] * 8,
        out_specs=VMEM,
        scratch_shapes=[
            pltpu.VMEM((PACK, BLOCK), jnp.float32),
            pltpu.VMEM((BLOCK, BLOCK), jnp.float32),
            pltpu.VMEM((BLOCK, BLOCK), jnp.float32),
            pltpu.VMEM((BLOCK, BLOCK), half),
        ],
        compiler_params=PARAMS,
        name="newton",
    )(info, *members)

    mine = [inverse] + [move(inverse, across_groups(shift)) for shift in range(1, RING)]
    others = [move(block, other_core) for block in mine]
    return tuple(
        pl.pallas_call(
            apply_kernel,
            out_shape=[shape(grad_qkv.shape), shape(grad_up.shape)],
            in_specs=[SMEM, VMEM, VMEM] + [ANY] * 8,
            out_specs=[VMEM] * 2,
            scratch_shapes=[
                pltpu.VMEM((8, PACK, BLOCK), half),
                pltpu.VMEM((BLOCK, BLOCK), half),
                pltpu.SemaphoreType.DMA((8,)),
            ],
            compiler_params=PARAMS,
            name="apply",
        )(info, grad_qkv, grad_up, *mine, *others)
    )


def solution(mesh):
    placed = (
        P(None, None, ("dp", "tensor"), None),
        P(None, "dp", "tensor"),
        P(None, "dp", "tensor"),
        P(),
    )
    return jax.shard_map(
        local,
        mesh=mesh,
        in_specs=placed,
        out_specs=(P(None, "dp", "tensor"), P(None, "dp", "tensor")),
        check_vma=False,
    )
```

```python
import functools

import jax
import jax.numpy as jnp
from jax import lax
from jax.experimental import pallas as pl
from jax.experimental.pallas import tpu as pltpu
from jax.sharding import PartitionSpec as P

DAMPING = 0.05
BLOCK = 640
TILE = 128
PACK = 384
PANELS = ((0, 0), (128, 0), (256, 0), (256, 384), (128, 512))
RING = 4
SLABS = 4
CHUNK = PACK // RING
PIECE = CHUNK // 2
AXES = ("dp", "tensor")
PARAMS = pltpu.CompilerParams(vmem_limit_bytes=48 * 1024 * 1024)
SMEM = pl.BlockSpec(memory_space=pltpu.SMEM)
VMEM = pl.BlockSpec(memory_space=pltpu.VMEM)
ANY = pl.BlockSpec(memory_space=pl.ANY)


def place_of(device):
    dp, t = device // 4, device % 4
    return dp // 32, dp // 8 % 4, dp // 2 % 4, dp % 2, t


def groups_by(key):
    found = {}
    for device in range(256):
        group, rank = key(*place_of(device))
        found.setdefault(group, []).append((rank, device))
    return [[device for _, device in sorted(found[group])] for group in sorted(found)]


def along_place(zl, x, y, c, t):
    return ((c, zl, y, t), x) if c == 0 else ((c, zl, x, t), y)


def across_place(zl, x, y, c, t):
    return ((c, zl, x, t), y) if c == 0 else ((c, zl, y, t), x)


def along_z(zl, x, y, c, t):
    return (x, y, c), 2 * t + zl


def sharing_block(zl, x, y, c, t):
    return ((c, x, t), 2 * y + zl) if c == 0 else ((c, y, t), 2 * x + zl)


def exchange(array, key):
    return lax.all_to_all(array, AXES, 0, 0, axis_index_groups=groups_by(key), tiled=True)


def to_other_core(array):
    return lax.ppermute(array, "dp", [(i, i ^ 1) for i in range(64)])


def pack_kernel(dev, act, own, sent, sem):
    core = dev[0] // 4 % 2
    copies = []
    for side, out in enumerate((sent, own)):
        for place in range(RING):
            for slab in range(SLABS):
                start = (2 * slab + place % 2) * BLOCK
                copies.append(
                    pltpu.make_async_copy(
                        act.at[core ^ (1 - side), place // 2, :, start : start + BLOCK],
                        out.at[place, slab],
                        sem.at[len(copies)],
                    )
                )
                copies[-1].start()
    for copy in copies:
        copy.wait()


def gram_kernel(own, other, out, tri):
    count = own.shape[0] * own.shape[2]
    for slab in range(SLABS):

        def product(low, high):
            def side(start, stop):
                return jnp.concatenate(
                    [
                        ref[:, slab, :, start:stop].reshape(count, stop - start)
                        for ref in (own, other)
                    ]
                )

            return lax.dot_general(
                side(low, high),
                side(low, BLOCK),
                (((0,), (0,)), ((), ())),
                preferred_element_type=jnp.float32,
            )

        top = product(0, 256)
        tri[0:128, :] = top[0:128]
        tri[128:256, 0:512] = top[128:256, 128:]
        middle = product(256, 512)
        tri[256:384, 0:384] = middle[0:128]
        tri[256:384, 384:640] = middle[128:256, 128:]
        tri[128:256, 512:640] = product(512, 640)
        for place in range(RING):
            rows = tri[place * CHUNK : (place + 1) * CHUNK, :]
            out[place, slab] = rows.astype(out.dtype)


def newton_kernel(tokens_all, dev, newton_steps, total, out, mixed, gap, mixed_half):
    dp, t = dev[0] // 4, dev[0] % 4
    core = dp % 2
    place = jnp.where(core == 0, dp // 8 % 4, dp // 2 % 4)
    steps = newton_steps[core, place // 2, 2 * t + place % 2]
    for i, (row, col) in enumerate(PANELS):
        low = TILE * i
        panel = total[row : row + TILE, col : col + BLOCK - low].astype(jnp.float32)
        mixed[low : low + TILE, low:] = panel
        if i < 4:
            mixed[low + TILE :, low : low + TILE] = panel[:, TILE:].T
    eye = (
        lax.broadcasted_iota(jnp.int32, (BLOCK, BLOCK), 0)
        == lax.broadcasted_iota(jnp.int32, (BLOCK, BLOCK), 1)
    ).astype(jnp.float32)
    factor = mixed[...] * (1.0 / tokens_all) + DAMPING * eye
    norm_scale = jnp.sqrt(jnp.sum(factor * factor))
    mixed[...] = factor / norm_scale

    def dot(a, b):
        return jnp.dot(a.astype(jnp.bfloat16), b, preferred_element_type=jnp.float32)

    gap[...] = mixed[...]
    power = 2.0
    for turn in range(1, 4):
        half = mixed[...].astype(jnp.bfloat16)
        mixed_half[...] = half
        mixed[...] = 2.0 * mixed[...] - dot(half, mixed_half[...])
        mixed_half[...] = mixed[...].astype(jnp.bfloat16)
        new_gap = 2.0 * gap[...] + power * mixed[...] - dot(gap[...], mixed_half[...])
        gap[...] = jnp.where(turn < steps, new_gap, gap[...])
        power = 2.0 * power
    reach = jnp.where(steps <= 1, 2.0, jnp.where(steps == 2, 4.0, jnp.where(steps == 3, 8.0, 16.0)))
    scale = 1.0 / norm_scale
    for i, (row, col) in enumerate(PANELS):
        low = TILE * i
        value = (reach * eye[low : low + TILE, low:] - gap[low : low + TILE, low:]) * scale
        for copy in range(RING):
            out[copy, row : row + TILE, col : col + BLOCK - low] = value.astype(jnp.bfloat16)


def apply_kernel(side, dev, blocks, grad_qkv, grad_up, *refs):
    outs, ins_here, outs_here = refs[-8:-6], refs[-6:-4], refs[-4:-2]
    whole, sem = refs[-2:]
    layer = (dev[0] // 4 % 2) ^ side
    loads = [
        pltpu.make_async_copy(grad.at[layer], here, sem.at[kind])
        for kind, (grad, here) in enumerate(zip((grad_qkv, grad_up), ins_here))
    ]
    stores = [
        pltpu.make_async_copy(here, out.at[layer], sem.at[2 + kind])
        for kind, (out, here) in enumerate(zip(outs, outs_here))
    ]
    for load in loads:
        load.start()
    for place in range(RING):
        kind, j = place // 2, place % 2
        for i, (row, col) in enumerate(PANELS):
            low = TILE * i
            panel = blocks[place, row : row + TILE, col : col + BLOCK - low]
            whole[place, low : low + TILE, low:] = panel
            if i < 4:
                whole[place, low + TILE :, low : low + TILE] = panel[:, TILE:].T
        if j == 0:
            loads[kind].wait()
        columns = slice(j * BLOCK, (j + 1) * BLOCK)
        outs_here[kind][:, columns] = jnp.dot(
            ins_here[kind][:, columns], whole[place], preferred_element_type=jnp.float32
        ).astype(jnp.bfloat16)
        if j == 1:
            stores[kind].start()
    for store in stores:
        store.wait()


def local(activations, grad_qkv, grad_up, newton_steps):
    half = jnp.bfloat16
    dev = (lax.axis_index("dp") * 4 + lax.axis_index("tensor")).astype(jnp.int32).reshape(1)
    rows = activations.shape[2]
    tokens_all = rows * 256

    def shape(*dims):
        return jax.ShapeDtypeStruct(dims, half)

    own, sent = pl.pallas_call(
        pack_kernel,
        out_shape=[shape(RING, SLABS, rows, BLOCK)] * 2,
        in_specs=[SMEM, ANY],
        out_specs=[ANY] * 2,
        scratch_shapes=[pltpu.SemaphoreType.DMA((2 * RING * SLABS,))],
        compiler_params=PARAMS,
        name="pack",
    )(dev, activations)
    other = to_other_core(sent)
    own = exchange(own, along_place)
    other = exchange(other, along_place)

    chunks = pl.pallas_call(
        gram_kernel,
        out_shape=shape(RING, SLABS, CHUNK, BLOCK),
        in_specs=[VMEM] * 2,
        out_specs=VMEM,
        scratch_shapes=[pltpu.VMEM((PACK, BLOCK), jnp.float32)],
        compiler_params=PARAMS,
        name="gram",
    )(own, other)
    chunks = exchange(chunks, across_place)
    pieces = jnp.sum(chunks.astype(jnp.float32), axis=0).astype(half)
    pieces = exchange(pieces.reshape(2 * SLABS, PIECE, BLOCK), along_z)
    piece = jnp.sum(pieces.astype(jnp.float32), axis=0).astype(half)
    members = jnp.broadcast_to(piece[None], (2 * RING, PIECE, BLOCK))
    total = exchange(members, sharing_block).reshape(PACK, BLOCK)

    inverse = pl.pallas_call(
        functools.partial(newton_kernel, tokens_all),
        out_shape=shape(RING, PACK, BLOCK),
        in_specs=[SMEM, SMEM, VMEM],
        out_specs=VMEM,
        scratch_shapes=[
            pltpu.VMEM((BLOCK, BLOCK), jnp.float32),
            pltpu.VMEM((BLOCK, BLOCK), jnp.float32),
            pltpu.VMEM((BLOCK, BLOCK), half),
        ],
        compiler_params=PARAMS,
        name="newton",
    )(dev, newton_steps, total)
    mine = exchange(inverse, along_place)
    others = to_other_core(mine)

    def apply(side, blocks, before):
        kinds = (grad_qkv.shape, grad_up.shape)
        here = [pltpu.VMEM(dims[1:], half) for dims in kinds]
        return pl.pallas_call(
            functools.partial(apply_kernel, side),
            out_shape=[shape(*dims) for dims in kinds],
            in_specs=[SMEM, VMEM] + [ANY] * (2 + len(before)),
            out_specs=[ANY] * 2,
            input_output_aliases={4: 0, 5: 1} if before else {},
            scratch_shapes=here
            + here
            + [pltpu.VMEM((RING, BLOCK, BLOCK), half), pltpu.SemaphoreType.DMA((4,))],
            compiler_params=PARAMS,
            name="apply",
        )(dev, blocks, grad_qkv, grad_up, *before)

    return tuple(apply(1, others, apply(0, mine, ())))


def solution(mesh):
    placed = (
        P(None, None, ("dp", "tensor"), None),
        P(None, "dp", "tensor"),
        P(None, "dp", "tensor"),
        P(),
    )
    return jax.shard_map(
        local,
        mesh=mesh,
        in_specs=placed,
        out_specs=(P(None, "dp", "tensor"), P(None, "dp", "tensor")),
        check_vma=False,
    )
```

```python
import functools

import jax
import jax.numpy as jnp
from jax import lax
from jax.experimental import pallas as pl
from jax.experimental.pallas import tpu as pltpu
from jax.sharding import PartitionSpec as P

DAMPING = 0.05
BLOCK = 640
TILE = 128
PACK = 384
PANELS = ((0, 0), (128, 0), (256, 0), (256, 384), (128, 512))
RING = 4
SLABS = 4
CHUNK = PACK // RING
PIECE = CHUNK // 2
AXES = ("dp", "tensor")
PARAMS = pltpu.CompilerParams(vmem_limit_bytes=48 * 1024 * 1024)
SMEM = pl.BlockSpec(memory_space=pltpu.SMEM)
VMEM = pl.BlockSpec(memory_space=pltpu.VMEM)
ANY = pl.BlockSpec(memory_space=pl.ANY)


def bit_a(i):
    return (i + 1) // 2 % 2


def bit_b(i):
    return i // 2


def device_at(device):
    dp, t = device // 4, device % 4
    return dp // 32, dp // 8 % 4, dp // 2 % 4, dp % 2, t


def squares(x, y, c):
    a, b = 2 * bit_a(x) + bit_a(y), 2 * bit_b(x) + bit_b(y)
    return (a, b) if c == 0 else (b, a)


def groups_by(key):
    found = {}
    for device in range(256):
        group, rank = key(*device_at(device))
        found.setdefault(group, []).append((rank, device))
    return [[device for _, device in sorted(found[group])] for group in sorted(found)]


def along_place(zl, x, y, c, t):
    place, other = squares(x, y, c)
    return (c, zl, t, other), place


def across_place(zl, x, y, c, t):
    place, other = squares(x, y, c)
    return (c, zl, t, place), other


def along_z(zl, x, y, c, t):
    return (x, y, c), 2 * t + zl


def sharing_block(zl, x, y, c, t):
    place, other = squares(x, y, c)
    return (c, t, place), 2 * other + zl


def exchange(array, key):
    return lax.all_to_all(array, AXES, 0, 0, axis_index_groups=groups_by(key), tiled=True)


def to_other_core(array):
    return lax.ppermute(array, "dp", [(i, i ^ 1) for i in range(64)])


def pack_kernel(dev, act, own, sent, sem):
    core = dev[0] // 4 % 2
    copies = []
    for side, out in enumerate((sent, own)):
        for place in range(RING):
            for slab in range(SLABS):
                start = (2 * slab + place % 2) * BLOCK
                copies.append(
                    pltpu.make_async_copy(
                        act.at[core ^ (1 - side), place // 2, :, start : start + BLOCK],
                        out.at[place, slab],
                        sem.at[len(copies)],
                    )
                )
                copies[-1].start()
    for copy in copies:
        copy.wait()


def gram_kernel(own, other, out, tri):
    count = own.shape[0] * own.shape[2]
    for slab in range(SLABS):

        def product(low, high):
            def side(start, stop):
                return jnp.concatenate(
                    [
                        ref[:, slab, :, start:stop].reshape(count, stop - start)
                        for ref in (own, other)
                    ]
                )

            return lax.dot_general(
                side(low, high),
                side(low, BLOCK),
                (((0,), (0,)), ((), ())),
                preferred_element_type=jnp.float32,
            )

        top = product(0, 256)
        tri[0:128, :] = top[0:128]
        tri[128:256, 0:512] = top[128:256, 128:]
        middle = product(256, 512)
        tri[256:384, 0:384] = middle[0:128]
        tri[256:384, 384:640] = middle[128:256, 128:]
        tri[128:256, 512:640] = product(512, 640)
        for place in range(RING):
            rows = tri[place * CHUNK : (place + 1) * CHUNK, :]
            out[place, slab] = rows.astype(out.dtype)


def newton_kernel(tokens_all, dev, newton_steps, total, out, mixed, gap, halves):
    dp, t = dev[0] // 4, dev[0] % 4
    core = dp % 2
    x, y = dp // 8 % 4, dp // 2 % 4
    place = jnp.where(core == 0, 2 * bit_a(x) + bit_a(y), 2 * bit_b(x) + bit_b(y))
    steps = newton_steps[core, place // 2, 2 * t + place % 2]
    for i, (row, col) in enumerate(PANELS):
        low = TILE * i
        panel = total[row : row + TILE, col : col + BLOCK - low].astype(jnp.float32)
        mixed[low : low + TILE, low:] = panel
        if i < 4:
            mixed[low + TILE :, low : low + TILE] = panel[:, TILE:].T
    eye = (
        lax.broadcasted_iota(jnp.int32, (BLOCK, BLOCK), 0)
        == lax.broadcasted_iota(jnp.int32, (BLOCK, BLOCK), 1)
    ).astype(jnp.float32)
    factor = mixed[...] * (1.0 / tokens_all) + DAMPING * eye
    norm_scale = jnp.sqrt(jnp.sum(factor * factor))
    mixed[...] = factor / norm_scale

    def dot(rows):
        return jnp.dot(halves[0:rows, :], halves[0:BLOCK, :], preferred_element_type=jnp.float32)

    def last():
        return jnp.dot(halves[BLOCK:, :], halves[0:BLOCK, :], preferred_element_type=jnp.float32)

    gap[...] = mixed[...]
    halves[0:BLOCK, :] = mixed[...].astype(jnp.bfloat16)
    halves[BLOCK:, :] = mixed[...].astype(jnp.bfloat16)
    mixed[...] = 2.0 * mixed[...] - dot(BLOCK)
    for turn in range(1, 4):
        halves[0:BLOCK, :] = mixed[...].astype(jnp.bfloat16)
        products = dot(2 * BLOCK) if turn < 3 else None
        step = products[BLOCK:] if turn < 3 else last()
        new_gap = 2.0 * gap[...] + 2.0**turn * mixed[...] - step
        gap[...] = jnp.where(turn < steps, new_gap, gap[...])
        if turn < 3:
            mixed[...] = 2.0 * mixed[...] - products[0:BLOCK]
            halves[BLOCK:, :] = gap[...].astype(jnp.bfloat16)
    reach = jnp.where(steps <= 1, 2.0, jnp.where(steps == 2, 4.0, jnp.where(steps == 3, 8.0, 16.0)))
    scale = 1.0 / norm_scale
    for i, (row, col) in enumerate(PANELS):
        low = TILE * i
        value = (reach * eye[low : low + TILE, low:] - gap[low : low + TILE, low:]) * scale
        for copy in range(RING):
            out[copy, row : row + TILE, col : col + BLOCK - low] = value.astype(jnp.bfloat16)


def apply_kernel(side, dev, blocks, grad_qkv, grad_up, *refs):
    outs, ins_here, outs_here = refs[-8:-6], refs[-6:-4], refs[-4:-2]
    whole, sem = refs[-2:]
    layer = (dev[0] // 4 % 2) ^ side
    loads = [
        pltpu.make_async_copy(grad.at[layer], here, sem.at[kind])
        for kind, (grad, here) in enumerate(zip((grad_qkv, grad_up), ins_here))
    ]
    stores = [
        pltpu.make_async_copy(here, out.at[layer], sem.at[2 + kind])
        for kind, (out, here) in enumerate(zip(outs, outs_here))
    ]
    for load in loads:
        load.start()
    for place in range(RING):
        kind, j = place // 2, place % 2
        for i, (row, col) in enumerate(PANELS):
            low = TILE * i
            panel = blocks[place, row : row + TILE, col : col + BLOCK - low]
            whole[place, low : low + TILE, low:] = panel
            if i < 4:
                whole[place, low + TILE :, low : low + TILE] = panel[:, TILE:].T
        if j == 0:
            loads[kind].wait()
        columns = slice(j * BLOCK, (j + 1) * BLOCK)
        outs_here[kind][:, columns] = jnp.dot(
            ins_here[kind][:, columns], whole[place], preferred_element_type=jnp.float32
        ).astype(jnp.bfloat16)
        if j == 1:
            stores[kind].start()
    for store in stores:
        store.wait()


def local(activations, grad_qkv, grad_up, newton_steps):
    half = jnp.bfloat16
    dev = (lax.axis_index("dp") * 4 + lax.axis_index("tensor")).astype(jnp.int32).reshape(1)
    rows = activations.shape[2]
    tokens_all = rows * 256

    def shape(*dims):
        return jax.ShapeDtypeStruct(dims, half)

    own, sent = pl.pallas_call(
        pack_kernel,
        out_shape=[shape(RING, SLABS, rows, BLOCK)] * 2,
        in_specs=[SMEM, ANY],
        out_specs=[ANY] * 2,
        scratch_shapes=[pltpu.SemaphoreType.DMA((2 * RING * SLABS,))],
        compiler_params=PARAMS,
        name="pack",
    )(dev, activations)
    other = to_other_core(sent)
    own = exchange(own, along_place)
    other = exchange(other, along_place)

    chunks = pl.pallas_call(
        gram_kernel,
        out_shape=shape(RING, SLABS, CHUNK, BLOCK),
        in_specs=[VMEM] * 2,
        out_specs=VMEM,
        scratch_shapes=[pltpu.VMEM((PACK, BLOCK), jnp.float32)],
        compiler_params=PARAMS,
        name="gram",
    )(own, other)
    chunks = exchange(chunks, across_place)
    pieces = jnp.sum(chunks.astype(jnp.float32), axis=0).astype(half)
    pieces = exchange(pieces.reshape(2 * SLABS, PIECE, BLOCK), along_z)
    piece = jnp.sum(pieces.astype(jnp.float32), axis=0).astype(half)
    members = jnp.broadcast_to(piece[None], (2 * RING, PIECE, BLOCK))
    total = exchange(members, sharing_block).reshape(PACK, BLOCK)

    inverse = pl.pallas_call(
        functools.partial(newton_kernel, tokens_all),
        out_shape=shape(RING, PACK, BLOCK),
        in_specs=[SMEM, SMEM, VMEM],
        out_specs=VMEM,
        scratch_shapes=[
            pltpu.VMEM((BLOCK, BLOCK), jnp.float32),
            pltpu.VMEM((BLOCK, BLOCK), jnp.float32),
            pltpu.VMEM((2 * BLOCK, BLOCK), half),
        ],
        compiler_params=PARAMS,
        name="newton",
    )(dev, newton_steps, total)
    mine = exchange(inverse, along_place)
    others = to_other_core(mine)

    def apply(side, blocks, before):
        kinds = (grad_qkv.shape, grad_up.shape)
        here = [pltpu.VMEM(dims[1:], half) for dims in kinds]
        return pl.pallas_call(
            functools.partial(apply_kernel, side),
            out_shape=[shape(*dims) for dims in kinds],
            in_specs=[SMEM, VMEM] + [ANY] * (2 + len(before)),
            out_specs=[ANY] * 2,
            input_output_aliases={4: 0, 5: 1} if before else {},
            scratch_shapes=here
            + here
            + [pltpu.VMEM((RING, BLOCK, BLOCK), half), pltpu.SemaphoreType.DMA((4,))],
            compiler_params=PARAMS,
            name="apply",
        )(dev, blocks, grad_qkv, grad_up, *before)

    return tuple(apply(1, others, apply(0, mine, ())))


def solution(mesh):
    placed = (
        P(None, None, ("dp", "tensor"), None),
        P(None, "dp", "tensor"),
        P(None, "dp", "tensor"),
        P(),
    )
    return jax.shard_map(
        local,
        mesh=mesh,
        in_specs=placed,
        out_specs=(P(None, "dp", "tensor"), P(None, "dp", "tensor")),
        check_vma=False,
    )
```

```python
import functools

import jax
import jax.numpy as jnp
from jax import lax
from jax.experimental import pallas as pl
from jax.experimental.pallas import tpu as pltpu
from jax.sharding import PartitionSpec as P

DAMPING = 0.05
BLOCK = 640
TILE = 128
PACK = 384
PANELS = ((0, 0), (128, 0), (256, 0), (256, 384), (128, 512))
RING = 4
SLABS = 4
CHUNK = PACK // RING
PIECE = CHUNK // 2
AXES = ("dp", "tensor")
PARAMS = pltpu.CompilerParams(vmem_limit_bytes=48 * 1024 * 1024)
SMEM = pl.BlockSpec(memory_space=pltpu.SMEM)
VMEM = pl.BlockSpec(memory_space=pltpu.VMEM)
ANY = pl.BlockSpec(memory_space=pl.ANY)


def bit_a(i):
    return (i + 1) // 2 % 2


def bit_b(i):
    return i // 2


def device_at(device):
    dp, t = device // 4, device % 4
    return dp // 32, dp // 8 % 4, dp // 2 % 4, dp % 2, t


def squares(x, y, c):
    a, b = 2 * bit_a(x) + bit_a(y), 2 * bit_b(x) + bit_b(y)
    return (a, b) if c == 0 else (b, a)


def groups_by(key):
    found = {}
    for device in range(256):
        group, rank = key(*device_at(device))
        found.setdefault(group, []).append((rank, device))
    return [[device for _, device in sorted(found[group])] for group in sorted(found)]


def along_z(zl, x, y, c, t):
    return (x, y, c), 2 * t + zl


def sharing_block(zl, x, y, c, t):
    place, other = squares(x, y, c)
    return (c, t, place), 2 * other + zl


def exchange(array, key):
    return lax.all_to_all(array, AXES, 0, 0, axis_index_groups=groups_by(key), tiled=True)


def to_other_core(array):
    return lax.ppermute(array, "dp", [(i, i ^ 1) for i in range(64)])


def in_square(array, flip, of_places):
    pairs = []
    for device in range(256):
        zl, x, y, c, t = device_at(device)
        if (c == 0) == of_places:
            x2, y2 = x ^ 1, y ^ 1
        else:
            x2, y2 = 3 - x, 3 - y
        x = x2 if flip & 2 else x
        y = y2 if flip & 1 else y
        pairs.append((device, (((zl * 4 + x) * 4 + y) * 2 + c) * 4 + t))
    return lax.ppermute(array, AXES, pairs)


def here(dev):
    dp = dev[0] // 4
    core, x, y = dp % 2, dp // 8 % 4, dp // 2 % 4
    a, b = 2 * bit_a(x) + bit_a(y), 2 * bit_b(x) + bit_b(y)
    return core, jnp.where(core == 0, a, b), jnp.where(core == 0, b, a)


def pack_kernel(side, dev, act, *refs):
    outs, sem = refs[:RING], refs[RING]
    core, mine, across = here(dev)
    copies = []
    for flip in range(RING):
        place = (across if side else mine) ^ flip
        for slab in range(SLABS):
            start = pl.multiple_of((2 * slab + place % 2) * BLOCK, TILE)
            copies.append(
                pltpu.make_async_copy(
                    act.at[core ^ side, place // 2, :, pl.ds(start, BLOCK)],
                    outs[flip].at[slab],
                    sem.at[len(copies)],
                )
            )
            copies[-1].start()
    for copy in copies:
        copy.wait()


def gram_kernel(dev, *refs):
    ins, outs, tri = refs[: 2 * RING], refs[2 * RING : 3 * RING], refs[3 * RING]
    across = here(dev)[2]
    for slab in range(SLABS):

        def product(low, high):
            return lax.dot_general(
                jnp.concatenate([ref[slab, :, low:high] for ref in ins]),
                jnp.concatenate([ref[slab, :, low:] for ref in ins]),
                (((0,), (0,)), ((), ())),
                preferred_element_type=jnp.float32,
            )

        top = product(0, 256)
        tri[0:128, :] = top[0:128]
        tri[128:256, 0:512] = top[128:256, 128:]
        middle = product(256, 512)
        tri[256:384, 0:384] = middle[0:128]
        tri[256:384, 384:640] = middle[128:256, 128:]
        tri[128:256, 512:640] = product(512, 640)
        for flip in range(RING):
            start = pl.multiple_of((across ^ flip) * CHUNK, 32)
            outs[flip][slab] = tri[pl.ds(start, CHUNK), :].astype(jnp.bfloat16)


def newton_kernel(tokens_all, dev, newton_steps, total, out, mixed, gap, halves):
    t = dev[0] % 4
    core, place, _ = here(dev)
    steps = newton_steps[core, place // 2, 2 * t + place % 2]
    for i, (row, col) in enumerate(PANELS):
        low = TILE * i
        panel = total[row : row + TILE, col : col + BLOCK - low].astype(jnp.float32)
        mixed[low : low + TILE, low:] = panel
        if i < 4:
            mixed[low + TILE :, low : low + TILE] = panel[:, TILE:].T
    eye = (
        lax.broadcasted_iota(jnp.int32, (BLOCK, BLOCK), 0)
        == lax.broadcasted_iota(jnp.int32, (BLOCK, BLOCK), 1)
    ).astype(jnp.float32)
    factor = mixed[...] * (1.0 / tokens_all) + DAMPING * eye
    norm_scale = jnp.sqrt(jnp.sum(factor * factor))
    mixed[...] = factor / norm_scale

    def dot(rows):
        return jnp.dot(halves[0:rows, :], halves[0:BLOCK, :], preferred_element_type=jnp.float32)

    def last():
        return jnp.dot(halves[BLOCK:, :], halves[0:BLOCK, :], preferred_element_type=jnp.float32)

    gap[...] = mixed[...]
    halves[0:BLOCK, :] = mixed[...].astype(jnp.bfloat16)
    halves[BLOCK:, :] = mixed[...].astype(jnp.bfloat16)
    mixed[...] = 2.0 * mixed[...] - dot(BLOCK)
    for turn in range(1, 4):
        halves[0:BLOCK, :] = mixed[...].astype(jnp.bfloat16)
        products = dot(2 * BLOCK) if turn < 3 else None
        step = products[BLOCK:] if turn < 3 else last()
        new_gap = 2.0 * gap[...] + 2.0**turn * mixed[...] - step
        gap[...] = jnp.where(turn < steps, new_gap, gap[...])
        if turn < 3:
            mixed[...] = 2.0 * mixed[...] - products[0:BLOCK]
            halves[BLOCK:, :] = gap[...].astype(jnp.bfloat16)
    reach = jnp.where(steps <= 1, 2.0, jnp.where(steps == 2, 4.0, jnp.where(steps == 3, 8.0, 16.0)))
    scale = 1.0 / norm_scale
    for i, (row, col) in enumerate(PANELS):
        low = TILE * i
        value = (reach * eye[low : low + TILE, low:] - gap[low : low + TILE, low:]) * scale
        out[row : row + TILE, col : col + BLOCK - low] = value.astype(jnp.bfloat16)


def apply_kernel(side, dev, *refs):
    ins, grads, outs = refs[:RING], refs[RING : RING + 2], refs[-10:-8]
    ins_here, outs_here, blocks, whole, sem, block_sem = refs[-8:-6], refs[-6:-4], *refs[-4:]
    core, mine, across = here(dev)
    layer = core ^ side
    arrivals = [
        pltpu.make_async_copy(
            ins[flip], blocks.at[(across if side else mine) ^ flip], block_sem.at[flip]
        )
        for flip in range(RING)
    ]
    loads = [
        pltpu.make_async_copy(grad.at[layer], place, sem.at[kind])
        for kind, (grad, place) in enumerate(zip(grads, ins_here))
    ]
    stores = [
        pltpu.make_async_copy(place, out.at[layer], sem.at[2 + kind])
        for kind, (out, place) in enumerate(zip(outs, outs_here))
    ]
    for copy in arrivals + loads:
        copy.start()
    for copy in arrivals:
        copy.wait()
    for place in range(RING):
        kind, j = place // 2, place % 2
        for i, (row, col) in enumerate(PANELS):
            low = TILE * i
            panel = blocks[place, row : row + TILE, col : col + BLOCK - low]
            whole[place, low : low + TILE, low:] = panel
            if i < 4:
                whole[place, low + TILE :, low : low + TILE] = panel[:, TILE:].T
        if j == 0:
            loads[kind].wait()
        columns = slice(j * BLOCK, (j + 1) * BLOCK)
        outs_here[kind][:, columns] = jnp.dot(
            ins_here[kind][:, columns], whole[place], preferred_element_type=jnp.float32
        ).astype(jnp.bfloat16)
        if j == 1:
            stores[kind].start()
    for store in stores:
        store.wait()


def local(activations, grad_qkv, grad_up, newton_steps):
    half = jnp.bfloat16
    dev = (lax.axis_index("dp") * 4 + lax.axis_index("tensor")).astype(jnp.int32).reshape(1)
    rows = activations.shape[2]
    tokens_all = rows * 256

    def shape(*dims):
        return jax.ShapeDtypeStruct(dims, half)

    def pack(side):
        return pl.pallas_call(
            functools.partial(pack_kernel, side),
            out_shape=[shape(SLABS, rows, BLOCK)] * RING,
            in_specs=[SMEM, ANY],
            out_specs=[ANY] * RING,
            scratch_shapes=[pltpu.SemaphoreType.DMA((RING * SLABS,))],
            compiler_params=PARAMS,
            name="pack",
        )(dev, activations)

    def over_square(parts, of_places):
        return [parts[0]] + [in_square(parts[flip], flip, of_places) for flip in (1, 2, 3)]

    own = pack(0)
    sent = pack(1)
    own = over_square(own, True)
    other = over_square([to_other_core(part) for part in sent], True)

    chunks = pl.pallas_call(
        gram_kernel,
        out_shape=[shape(SLABS, CHUNK, BLOCK)] * RING,
        in_specs=[SMEM] + [VMEM] * (2 * RING),
        out_specs=[VMEM] * RING,
        scratch_shapes=[pltpu.VMEM((PACK, BLOCK), jnp.float32)],
        compiler_params=PARAMS,
        name="gram",
    )(dev, *own, *other)
    chunks = over_square(chunks, False)
    pieces = sum(chunk.astype(jnp.float32) for chunk in chunks).astype(half)
    pieces = exchange(pieces.reshape(2 * SLABS, PIECE, BLOCK), along_z)
    piece = jnp.sum(pieces.astype(jnp.float32), axis=0).astype(half)
    members = jnp.broadcast_to(piece[None], (2 * RING, PIECE, BLOCK))
    total = exchange(members, sharing_block).reshape(PACK, BLOCK)

    inverse = pl.pallas_call(
        functools.partial(newton_kernel, tokens_all),
        out_shape=shape(PACK, BLOCK),
        in_specs=[SMEM, SMEM, VMEM],
        out_specs=VMEM,
        scratch_shapes=[
            pltpu.VMEM((BLOCK, BLOCK), jnp.float32),
            pltpu.VMEM((BLOCK, BLOCK), jnp.float32),
            pltpu.VMEM((2 * BLOCK, BLOCK), half),
        ],
        compiler_params=PARAMS,
        name="newton",
    )(dev, newton_steps, total)
    mine = over_square([inverse] * RING, True)
    others = [to_other_core(block) for block in mine]

    def apply(side, blocks, before):
        kinds = (grad_qkv.shape, grad_up.shape)
        buffers = [pltpu.VMEM(dims[1:], half) for dims in kinds]
        return pl.pallas_call(
            functools.partial(apply_kernel, side),
            out_shape=[shape(*dims) for dims in kinds],
            in_specs=[SMEM] + [ANY] * (RING + 2 + len(before)),
            out_specs=[ANY] * 2,
            input_output_aliases={7: 0, 8: 1} if before else {},
            scratch_shapes=buffers
            + buffers
            + [
                pltpu.VMEM((RING, PACK, BLOCK), half),
                pltpu.VMEM((RING, BLOCK, BLOCK), half),
                pltpu.SemaphoreType.DMA((4,)),
                pltpu.SemaphoreType.DMA((RING,)),
            ],
            compiler_params=PARAMS,
            name="apply",
        )(dev, *blocks, grad_qkv, grad_up, *before)

    return tuple(apply(1, others, apply(0, mine, ())))


def solution(mesh):
    placed = (
        P(None, None, ("dp", "tensor"), None),
        P(None, "dp", "tensor"),
        P(None, "dp", "tensor"),
        P(),
    )
    return jax.shard_map(
        local,
        mesh=mesh,
        in_specs=placed,
        out_specs=(P(None, "dp", "tensor"), P(None, "dp", "tensor")),
        check_vma=False,
    )
```

```python
import functools

import jax
import jax.numpy as jnp
from jax import lax
from jax.experimental import pallas as pl
from jax.experimental.pallas import tpu as pltpu
from jax.sharding import PartitionSpec as P

DAMPING = 0.05
BLOCK = 640
TILE = 128
PACK = 384
PANELS = ((0, 0), (128, 0), (256, 0), (256, 384), (128, 512))
RING = 4
SLABS = 4
CHUNK = PACK // RING
AXES = ("dp", "tensor")
PARAMS = pltpu.CompilerParams(vmem_limit_bytes=24 * 1024 * 1024)
SMEM = pl.BlockSpec(memory_space=pltpu.SMEM)
VMEM = pl.BlockSpec(memory_space=pltpu.VMEM)
ANY = pl.BlockSpec(memory_space=pl.ANY)


def bit_a(i):
    return (i + 1) // 2 % 2


def bit_b(i):
    return i // 2


def device_at(device):
    dp, t = device // 4, device % 4
    return dp // 32, dp // 8 % 4, dp // 2 % 4, dp % 2, t


def move(array, target):
    pairs = []
    for device in range(256):
        zl, x, y, c, t = target(*device_at(device))
        pairs.append((device, (((zl * 4 + x) * 4 + y) * 2 + c) * 4 + t))
    return lax.ppermute(array, AXES, pairs)


def to_other_core(array):
    return move(array, lambda zl, x, y, c, t: (zl, x, y, 1 - c, t))


def in_square(array, flip, of_places):
    def target(zl, x, y, c, t):
        x2, y2 = (x ^ 1, y ^ 1) if (c == 0) == of_places else (3 - x, 3 - y)
        return zl, x2 if flip & 2 else x, y2 if flip & 1 else y, c, t

    return move(array, target)


def to_slab(array, step):
    return move(array, lambda zl, x, y, c, t: (zl, x, y, c, t ^ 1 if c == step else 3 - t))


def to_z_neighbour(array):
    return move(array, lambda zl, x, y, c, t: (1 - zl, x, y, c, t))


def here(dev):
    dp = dev[0] // 4
    core, x, y = dp % 2, dp // 8 % 4, dp // 2 % 4
    a, b = 2 * bit_a(x) + bit_a(y), 2 * bit_b(x) + bit_b(y)
    return core, jnp.where(core == 0, a, b), jnp.where(core == 0, b, a)


def pack_kernel(dev, act, own_0, own_1, own_2, own_3, diagonal, rest, sem):
    core, mine, across = here(dev)
    t = dev[0] % 4
    copies = []
    for side, outs in (
        (1, (rest.at[0], rest.at[1], rest.at[2], diagonal)),
        (0, (own_0, own_1, own_2, own_3)),
    ):
        first = jnp.where(core == side, t ^ 1, 3 - t)
        second = jnp.where(core == side, 3 - t, t ^ 1)
        for flip, out in enumerate(outs):
            place = (across if side else mine) ^ flip
            for rank, slab in enumerate((t, second, first, t ^ 2)):
                start = pl.multiple_of((2 * slab + place % 2) * BLOCK, TILE)
                copies.append(
                    pltpu.make_async_copy(
                        act.at[core ^ side, place // 2, :, pl.ds(start, BLOCK)],
                        out.at[rank],
                        sem.at[len(copies)],
                    )
                )
                copies[-1].start()
    for copy in copies:
        copy.wait()


def gram_kernel(dev, *refs):
    ins, outs, tri = refs[: 2 * RING], refs[2 * RING : 3 * RING], refs[3 * RING]
    ins = [*ins[:-1], ins[-1].at[0]]
    across = here(dev)[2]
    for slab in range(SLABS):

        def product(low, high):
            return lax.dot_general(
                jnp.concatenate([ref[slab, :, low:high] for ref in ins]),
                jnp.concatenate([ref[slab, :, low:] for ref in ins]),
                (((0,), (0,)), ((), ())),
                preferred_element_type=jnp.float32,
            )

        top = product(0, 256)
        tri[0:128, :] = top[0:128]
        tri[128:256, 0:512] = top[128:256, 128:]
        middle = product(256, 512)
        tri[256:384, 0:384] = middle[0:128]
        tri[256:384, 384:640] = middle[128:256, 128:]
        tri[128:256, 512:640] = product(512, 640)
        for flip in range(RING):
            start = pl.multiple_of((across ^ flip) * CHUNK, 32)
            outs[flip][slab] = tri[pl.ds(start, CHUNK), :].astype(jnp.bfloat16)


def newton_kernel(tokens_all, dev, newton_steps, *refs):
    ins, (out, total, mixed, gap, halves) = refs[:RING], refs[RING:]
    t = dev[0] % 4
    core, place, across = here(dev)
    for flip in range(RING):
        start = pl.multiple_of((across ^ flip) * CHUNK, 32)
        total[pl.ds(start, CHUNK), :] = ins[3 - flip][...].astype(jnp.float32)
    steps = newton_steps[core, place // 2, 2 * t + place % 2]
    for i, (row, col) in enumerate(PANELS):
        low = TILE * i
        panel = total[row : row + TILE, col : col + BLOCK - low]
        mixed[low : low + TILE, low:] = panel
        if i < 4:
            mixed[low + TILE :, low : low + TILE] = panel[:, TILE:].T
    eye = (
        lax.broadcasted_iota(jnp.int32, (BLOCK, BLOCK), 0)
        == lax.broadcasted_iota(jnp.int32, (BLOCK, BLOCK), 1)
    ).astype(jnp.float32)
    factor = mixed[...] * (1.0 / tokens_all) + DAMPING * eye
    norm_scale = jnp.sqrt(jnp.sum(factor * factor))
    mixed[...] = factor / norm_scale

    def dot(rows):
        return jnp.dot(halves[0:rows, :], halves[0:BLOCK, :], preferred_element_type=jnp.float32)

    def last():
        return jnp.dot(halves[BLOCK:, :], halves[0:BLOCK, :], preferred_element_type=jnp.float32)

    gap[...] = mixed[...]
    halves[0:BLOCK, :] = mixed[...].astype(jnp.bfloat16)
    halves[BLOCK:, :] = mixed[...].astype(jnp.bfloat16)
    mixed[...] = 2.0 * mixed[...] - dot(BLOCK)
    for turn in range(1, 4):
        halves[0:BLOCK, :] = mixed[...].astype(jnp.bfloat16)
        products = dot(2 * BLOCK) if turn < 3 else None
        step = products[BLOCK:] if turn < 3 else last()
        new_gap = 2.0 * gap[...] + 2.0**turn * mixed[...] - step
        gap[...] = jnp.where(turn < steps, new_gap, gap[...])
        if turn < 3:
            mixed[...] = 2.0 * mixed[...] - products[0:BLOCK]
            halves[BLOCK:, :] = gap[...].astype(jnp.bfloat16)
    reach = jnp.where(steps <= 1, 2.0, jnp.where(steps == 2, 4.0, jnp.where(steps == 3, 8.0, 16.0)))
    scale = 1.0 / norm_scale
    for i, (row, col) in enumerate(PANELS):
        low = TILE * i
        value = (reach * eye[low : low + TILE, low:] - gap[low : low + TILE, low:]) * scale
        out[row : row + TILE, col : col + BLOCK - low] = value.astype(jnp.bfloat16)


def apply_kernel(side, dev, *refs):
    ins, grads, outs = refs[:RING], refs[RING : RING + 2], refs[-8:-6]
    ins_here, outs_here, whole, sem = refs[-6:-4], refs[-4:-2], refs[-2], refs[-1]
    core, mine, across = here(dev)
    layer = core ^ side
    mine = across if side else mine
    loads = [
        pltpu.make_async_copy(grad.at[layer], place, sem.at[kind])
        for kind, (grad, place) in enumerate(zip(grads, ins_here))
    ]
    stores = [
        pltpu.make_async_copy(place, out.at[layer], sem.at[2 + kind])
        for kind, (out, place) in enumerate(zip(outs, outs_here))
    ]
    for load in loads:
        load.start()

    def unfold(block, place):
        for i, (row, col) in enumerate(PANELS):
            low = TILE * i
            panel = block[row : row + TILE, col : col + BLOCK - low]
            whole[place, low : low + TILE, low:] = panel
            if i < 4:
                whole[place, low + TILE :, low : low + TILE] = panel[:, TILE:].T

    for flip in range(RING):
        unfold(ins[flip], mine ^ flip)
    for place in range(RING):
        kind, j = place // 2, place % 2
        if j == 0:
            loads[kind].wait()
        columns = slice(j * BLOCK, (j + 1) * BLOCK)
        outs_here[kind][:, columns] = jnp.dot(
            ins_here[kind][:, columns], whole[place], preferred_element_type=jnp.float32
        ).astype(jnp.bfloat16)
        if j == 1:
            stores[kind].start()
    for store in stores:
        store.wait()


def local(activations, grad_qkv, grad_up, newton_steps):
    half = jnp.bfloat16
    dev = (lax.axis_index("dp") * 4 + lax.axis_index("tensor")).astype(jnp.int32).reshape(1)
    rows = activations.shape[2]
    tokens_all = rows * 256

    def shape(*dims):
        return jax.ShapeDtypeStruct(dims, half)

    def over_square(parts, of_places):
        moved = {flip: in_square(parts[flip], flip, of_places) for flip in (3, 2, 1)}
        return [parts[0]] + [moved[flip] for flip in (1, 2, 3)]

    part = (SLABS, rows, BLOCK)
    *own, diagonal, rest = pl.pallas_call(
        pack_kernel,
        out_shape=[shape(*part)] * (RING + 1) + [shape(3, *part)],
        in_specs=[SMEM, ANY],
        out_specs=[ANY] * (RING + 2),
        scratch_shapes=[pltpu.SemaphoreType.DMA((2 * RING * SLABS,))],
        compiler_params=pltpu.CompilerParams(vmem_limit_bytes=48 * 1024 * 1024),
        name="pack",
    )(dev, activations)
    own = over_square(own, True)
    diagonal, rest = to_other_core(diagonal), to_other_core(rest)
    diagonal = in_square(diagonal, 3, True)
    others = [in_square(rest[flip], flip, True) for flip in (2, 1)]

    chunks = pl.pallas_call(
        gram_kernel,
        out_shape=[shape(SLABS, CHUNK, BLOCK)] * RING,
        in_specs=[SMEM] + [VMEM] * (2 * RING),
        out_specs=[VMEM] * RING,
        scratch_shapes=[pltpu.VMEM((PACK, BLOCK), jnp.float32)],
        compiler_params=PARAMS,
        name="gram",
    )(dev, *own[::-1], diagonal, *others, rest)
    chunks = over_square(chunks, False)

    def wide(array):
        return array.astype(jnp.float32)

    sums = sum(wide(chunk) for chunk in chunks[::-1])
    sums = sums[0:2] + wide(to_slab(sums[2:4].astype(half), 0))
    sums = sums[0] + wide(to_slab(sums[1].astype(half), 1))
    sums = sums + wide(to_z_neighbour(sums.astype(half)))
    members = over_square([sums.astype(half)] * RING, False)

    inverse = pl.pallas_call(
        functools.partial(newton_kernel, tokens_all),
        out_shape=shape(PACK, BLOCK),
        in_specs=[SMEM, SMEM] + [VMEM] * RING,
        out_specs=VMEM,
        scratch_shapes=[
            pltpu.VMEM((PACK, BLOCK), jnp.float32),
            pltpu.VMEM((BLOCK, BLOCK), jnp.float32),
            pltpu.VMEM((BLOCK, BLOCK), jnp.float32),
            pltpu.VMEM((2 * BLOCK, BLOCK), half),
        ],
        compiler_params=PARAMS,
        name="newton",
    )(dev, newton_steps, *members[::-1])
    mine = over_square([inverse] * RING, True)
    others = [to_other_core(block) for block in mine]

    def apply(side, blocks, before):
        kinds = (grad_qkv.shape, grad_up.shape)
        buffers = [pltpu.VMEM(dims[1:], half) for dims in kinds]
        return pl.pallas_call(
            functools.partial(apply_kernel, side),
            out_shape=[shape(*dims) for dims in kinds],
            in_specs=[SMEM] + [VMEM] * RING + [ANY] * (2 + len(before)),
            out_specs=[ANY] * 2,
            input_output_aliases={7: 0, 8: 1} if before else {},
            scratch_shapes=buffers
            + buffers
            + [
                pltpu.VMEM((RING, BLOCK, BLOCK), half),
                pltpu.SemaphoreType.DMA((4,)),
            ],
            compiler_params=PARAMS,
            name="apply",
        )(dev, *blocks, grad_qkv, grad_up, *before)

    return tuple(apply(1, others, apply(0, mine, ())))


def solution(mesh):
    placed = (
        P(None, None, ("dp", "tensor"), None),
        P(None, "dp", "tensor"),
        P(None, "dp", "tensor"),
        P(),
    )
    return jax.shard_map(
        local,
        mesh=mesh,
        in_specs=placed,
        out_specs=(P(None, "dp", "tensor"), P(None, "dp", "tensor")),
        check_vma=False,
    )
```

```python
import functools

import jax
import jax.numpy as jnp
from jax import lax
from jax.experimental import pallas as pl
from jax.experimental.pallas import tpu as pltpu
from jax.sharding import PartitionSpec as P

DAMPING = 0.05
BLOCK = 640
TILE = 128
PACK = 384
PANELS = ((0, 0), (128, 0), (256, 0), (256, 384), (128, 512))
RING = 4
SLABS = 4
CHUNK = PACK // RING
AXES = ("dp", "tensor")
PARAMS = pltpu.CompilerParams(vmem_limit_bytes=24 * 1024 * 1024)
SMEM = pl.BlockSpec(memory_space=pltpu.SMEM)
VMEM = pl.BlockSpec(memory_space=pltpu.VMEM)
ANY = pl.BlockSpec(memory_space=pl.ANY)


def bit_a(i):
    return (i + 1) // 2 % 2


def bit_b(i):
    return i // 2


def device_at(device):
    dp, t = device // 4, device % 4
    return dp // 32, dp // 8 % 4, dp // 2 % 4, dp % 2, t


def move(array, target):
    pairs = []
    for device in range(256):
        zl, x, y, c, t = target(*device_at(device))
        pairs.append((device, (((zl * 4 + x) * 4 + y) * 2 + c) * 4 + t))
    return lax.ppermute(array, AXES, pairs)


def to_other_core(array):
    return move(array, lambda zl, x, y, c, t: (zl, x, y, 1 - c, t))


def in_square(array, flip, of_places):
    def target(zl, x, y, c, t):
        x2, y2 = (x ^ 1, y ^ 1) if (c == 0) == of_places else (3 - x, 3 - y)
        return zl, x2 if flip & 2 else x, y2 if flip & 1 else y, c, t

    return move(array, target)


def to_slab(array, step):
    return move(array, lambda zl, x, y, c, t: (zl, x, y, c, t ^ 1 if c == step else 3 - t))


def to_z_neighbour(array):
    return move(array, lambda zl, x, y, c, t: (1 - zl, x, y, c, t))


def here(dev):
    dp = dev[0] // 4
    core, x, y = dp % 2, dp // 8 % 4, dp // 2 % 4
    a, b = 2 * bit_a(x) + bit_a(y), 2 * bit_b(x) + bit_b(y)
    return core, jnp.where(core == 0, a, b), jnp.where(core == 0, b, a)


def pack_kernel(dev, act, *refs):
    outs, sem = refs[:-1], refs[-1]
    core, mine, across = here(dev)
    t = dev[0] % 4
    copies = []
    for half in range(2):
        *own, sent = outs[(RING + 1) * half : (RING + 1) * (half + 1)]
        for side in (1, 0):
            first = jnp.where(core == side, t ^ 1, 3 - t)
            second = jnp.where(core == side, 3 - t, t ^ 1)
            for flip in range(RING):
                place = (across if side else mine) ^ flip
                for rank, slab in enumerate((t, second) if half else (first, t ^ 2)):
                    start = pl.multiple_of((2 * slab + place % 2) * BLOCK, TILE)
                    copies.append(
                        pltpu.make_async_copy(
                            act.at[core ^ side, place // 2, :, pl.ds(start, BLOCK)],
                            (sent.at[flip] if side else own[flip]).at[rank],
                            sem.at[len(copies)],
                        )
                    )
                    copies[-1].start()
    for copy in copies:
        copy.wait()


def gram_kernel(dev, *refs):
    ins, outs, tri = refs[: 2 * RING], refs[2 * RING : 3 * RING], refs[3 * RING]
    ins = [*ins[:-1], ins[-1].at[0]]
    across = here(dev)[2]
    for slab in range(2):

        def product(low, high):
            return lax.dot_general(
                jnp.concatenate([ref[slab, :, low:high] for ref in ins]),
                jnp.concatenate([ref[slab, :, low:] for ref in ins]),
                (((0,), (0,)), ((), ())),
                preferred_element_type=jnp.float32,
            )

        top = product(0, 256)
        tri[0:128, :] = top[0:128]
        tri[128:256, 0:512] = top[128:256, 128:]
        middle = product(256, 512)
        tri[256:384, 0:384] = middle[0:128]
        tri[256:384, 384:640] = middle[128:256, 128:]
        tri[128:256, 512:640] = product(512, 640)
        for flip in range(RING):
            start = pl.multiple_of((across ^ flip) * CHUNK, 32)
            outs[flip][slab] = tri[pl.ds(start, CHUNK), :].astype(jnp.bfloat16)


def newton_kernel(tokens_all, dev, newton_steps, *refs):
    ins, (out, total, mixed, gap, halves) = refs[:RING], refs[RING:]
    t = dev[0] % 4
    core, place, across = here(dev)
    for flip in range(RING):
        start = pl.multiple_of((across ^ flip) * CHUNK, 32)
        total[pl.ds(start, CHUNK), :] = ins[3 - flip][...]
    steps = newton_steps[core, place // 2, 2 * t + place % 2]
    eye = (
        lax.broadcasted_iota(jnp.int32, (BLOCK, BLOCK), 0)
        == lax.broadcasted_iota(jnp.int32, (BLOCK, BLOCK), 1)
    ).astype(jnp.float32)
    squares = jnp.zeros((TILE, TILE), jnp.float32)
    for i, (row, col) in enumerate(PANELS):
        low = TILE * i
        panel = total[row : row + TILE, col : col + BLOCK - low]
        for j in range(i, 5):
            tile = panel[:, TILE * (j - i) : TILE * (j - i + 1)].astype(jnp.float32)
            tile = tile * (1.0 / tokens_all)
            if i == j:
                tile = tile + DAMPING * eye[:TILE, :TILE]
            mixed[low : low + TILE, TILE * j : TILE * (j + 1)] = tile
            squares = squares + (1.0 if i == j else 2.0) * tile * tile
            if i != j:
                mixed[TILE * j : TILE * (j + 1), low : low + TILE] = tile.T
    norm_scale = jnp.sqrt(jnp.sum(squares))
    scale = 1.0 / norm_scale

    def dot(rows):
        return jnp.dot(halves[0:rows, :], halves[0:BLOCK, :], preferred_element_type=jnp.float32)

    def last():
        return jnp.dot(halves[BLOCK:, :], halves[0:BLOCK, :], preferred_element_type=jnp.float32)

    start = mixed[...] * scale
    gap[...] = start
    halves[0:BLOCK, :] = start.astype(jnp.bfloat16)
    halves[BLOCK:, :] = start.astype(jnp.bfloat16)
    mixed[...] = 2.0 * gap[...] - dot(BLOCK)
    for turn in range(1, 4):
        halves[0:BLOCK, :] = mixed[...].astype(jnp.bfloat16)
        products = dot(2 * BLOCK) if turn < 3 else None
        step = products[BLOCK:] if turn < 3 else last()
        new_gap = 2.0 * gap[...] + 2.0**turn * mixed[...] - step
        gap[...] = jnp.where(turn < steps, new_gap, gap[...])
        if turn < 3:
            mixed[...] = 2.0 * mixed[...] - products[0:BLOCK]
            halves[BLOCK:, :] = gap[...].astype(jnp.bfloat16)
    reach = jnp.where(steps <= 1, 2.0, jnp.where(steps == 2, 4.0, jnp.where(steps == 3, 8.0, 16.0)))
    for i, (row, col) in enumerate(PANELS):
        low = TILE * i
        value = (reach * eye[low : low + TILE, low:] - gap[low : low + TILE, low:]) * scale
        out[row : row + TILE, col : col + BLOCK - low] = value.astype(jnp.bfloat16)


def apply_kernel(side, dev, *refs):
    ins, grads, outs = refs[:RING], refs[RING : RING + 2], refs[-8:-6]
    ins_here, outs_here, whole, sem = refs[-6:-4], refs[-4:-2], refs[-2], refs[-1]
    core, mine, across = here(dev)
    layer = core ^ side
    mine = across if side else mine
    loads = [
        pltpu.make_async_copy(grad.at[layer], place, sem.at[kind])
        for kind, (grad, place) in enumerate(zip(grads, ins_here))
    ]
    stores = [
        pltpu.make_async_copy(place, out.at[layer], sem.at[2 + kind])
        for kind, (out, place) in enumerate(zip(outs, outs_here))
    ]
    for load in loads:
        load.start()

    def unfold(block, place):
        for i, (row, col) in enumerate(PANELS):
            low = TILE * i
            panel = block[row : row + TILE, col : col + BLOCK - low]
            whole[place, low : low + TILE, low:] = panel
            if i < 4:
                whole[place, low + TILE :, low : low + TILE] = panel[:, TILE:].T

    for flip in range(RING):
        unfold(ins[flip], mine ^ flip)
    for place in range(RING):
        kind, j = place // 2, place % 2
        if j == 0:
            loads[kind].wait()
        columns = slice(j * BLOCK, (j + 1) * BLOCK)
        outs_here[kind][:, columns] = jnp.dot(
            ins_here[kind][:, columns], whole[place], preferred_element_type=jnp.float32
        ).astype(jnp.bfloat16)
        if j == 1:
            stores[kind].start()
    for store in stores:
        store.wait()


def local(activations, grad_qkv, grad_up, newton_steps):
    half = jnp.bfloat16
    dev = (lax.axis_index("dp") * 4 + lax.axis_index("tensor")).astype(jnp.int32).reshape(1)
    rows = activations.shape[2]
    tokens_all = rows * 256

    def shape(*dims):
        return jax.ShapeDtypeStruct(dims, half)

    def wide(array):
        return array.astype(jnp.float32)

    def over_square(parts, of_places):
        moved = {flip: in_square(parts[flip], flip, of_places) for flip in (3, 2, 1)}
        return [parts[0]] + [moved[flip] for flip in (1, 2, 3)]

    part = (2, rows, BLOCK)
    packed = pl.pallas_call(
        pack_kernel,
        out_shape=([shape(*part)] * RING + [shape(RING, *part)]) * 2,
        in_specs=[SMEM, ANY],
        out_specs=[ANY] * (2 * RING + 2),
        scratch_shapes=[pltpu.SemaphoreType.DMA((4 * RING * 2,))],
        compiler_params=pltpu.CompilerParams(vmem_limit_bytes=48 * 1024 * 1024),
        name="pack",
    )(dev, activations)

    def factors(own, sent):
        received = to_other_core(sent)
        own = over_square(own, True)
        others = [in_square(received[flip], flip, True) for flip in (3, 2, 1)]
        chunks = pl.pallas_call(
            gram_kernel,
            out_shape=[shape(2, CHUNK, BLOCK)] * RING,
            in_specs=[SMEM] + [VMEM] * (2 * RING),
            out_specs=[VMEM] * RING,
            scratch_shapes=[pltpu.VMEM((PACK, BLOCK), jnp.float32)],
            compiler_params=PARAMS,
            name="gram",
        )(dev, *own[::-1], *others, received)
        chunks = over_square(chunks, False)
        return sum(wide(chunk) for chunk in chunks[::-1])

    leaving = to_slab(factors(packed[:RING], packed[RING]).astype(half), 0)
    sums = factors(packed[RING + 1 : -1], packed[-1]) + wide(leaving)
    sums = sums[0] + wide(to_slab(sums[1].astype(half), 1))
    sums = sums + wide(to_z_neighbour(sums.astype(half)))
    members = over_square([sums.astype(half)] * RING, False)

    inverse = pl.pallas_call(
        functools.partial(newton_kernel, tokens_all),
        out_shape=shape(PACK, BLOCK),
        in_specs=[SMEM, SMEM] + [VMEM] * RING,
        out_specs=VMEM,
        scratch_shapes=[
            pltpu.VMEM((PACK, BLOCK), half),
            pltpu.VMEM((BLOCK, BLOCK), jnp.float32),
            pltpu.VMEM((BLOCK, BLOCK), jnp.float32),
            pltpu.VMEM((2 * BLOCK, BLOCK), half),
        ],
        compiler_params=PARAMS,
        name="newton",
    )(dev, newton_steps, *members[::-1])
    mine = over_square([inverse] * RING, True)
    others = [to_other_core(block) for block in mine]

    def apply(side, blocks, before):
        kinds = (grad_qkv.shape, grad_up.shape)
        buffers = [pltpu.VMEM(dims[1:], half) for dims in kinds]
        return pl.pallas_call(
            functools.partial(apply_kernel, side),
            out_shape=[shape(*dims) for dims in kinds],
            in_specs=[SMEM] + [VMEM] * RING + [ANY] * (2 + len(before)),
            out_specs=[ANY] * 2,
            input_output_aliases={7: 0, 8: 1} if before else {},
            scratch_shapes=buffers
            + buffers
            + [
                pltpu.VMEM((RING, BLOCK, BLOCK), half),
                pltpu.SemaphoreType.DMA((4,)),
            ],
            compiler_params=PARAMS,
            name="apply",
        )(dev, *blocks, grad_qkv, grad_up, *before)

    return tuple(apply(1, others, apply(0, mine, ())))


def solution(mesh):
    placed = (
        P(None, None, ("dp", "tensor"), None),
        P(None, "dp", "tensor"),
        P(None, "dp", "tensor"),
        P(),
    )
    return jax.shard_map(
        local,
        mesh=mesh,
        in_specs=placed,
        out_specs=(P(None, "dp", "tensor"), P(None, "dp", "tensor")),
        check_vma=False,
    )
```

```python
import functools

import jax
import jax.numpy as jnp
from jax import lax
from jax.experimental import pallas as pl
from jax.experimental.pallas import tpu as pltpu
from jax.sharding import PartitionSpec as P

DAMPING = 0.05
BLOCK = 640
TILE = 128
PACK = 384
PANELS = ((0, 0), (128, 0), (256, 0), (256, 384), (128, 512))
RING = 4
SLABS = 4
CHUNK = PACK // RING
AXES = ("dp", "tensor")
PARAMS = pltpu.CompilerParams(vmem_limit_bytes=24 * 1024 * 1024)
SMEM = pl.BlockSpec(memory_space=pltpu.SMEM)
VMEM = pl.BlockSpec(memory_space=pltpu.VMEM)
ANY = pl.BlockSpec(memory_space=pl.ANY)


def bit_a(i):
    return (i + 1) // 2 % 2


def bit_b(i):
    return i // 2


def device_at(device):
    dp, t = device // 4, device % 4
    return dp // 32, dp // 8 % 4, dp // 2 % 4, dp % 2, t


def move(array, target):
    pairs = []
    for device in range(256):
        zl, x, y, c, t = target(*device_at(device))
        pairs.append((device, (((zl * 4 + x) * 4 + y) * 2 + c) * 4 + t))
    return lax.ppermute(array, AXES, pairs)


def to_other_core(array):
    return move(array, lambda zl, x, y, c, t: (zl, x, y, 1 - c, t))


def in_square(array, flip, of_places):
    def target(zl, x, y, c, t):
        x2, y2 = (x ^ 1, y ^ 1) if (c == 0) == of_places else (3 - x, 3 - y)
        return zl, x2 if flip & 2 else x, y2 if flip & 1 else y, c, t

    return move(array, target)


def to_slab(array, step):
    return move(array, lambda zl, x, y, c, t: (zl, x, y, c, t ^ 1 if c == step else 3 - t))


def to_z_neighbour(array):
    return move(array, lambda zl, x, y, c, t: (1 - zl, x, y, c, t))


def here(dev):
    dp = dev[0] // 4
    core, x, y = dp % 2, dp // 8 % 4, dp // 2 % 4
    a, b = 2 * bit_a(x) + bit_a(y), 2 * bit_b(x) + bit_b(y)
    return core, jnp.where(core == 0, a, b), jnp.where(core == 0, b, a)


def pack_kernel(dev, act, *refs):
    outs, sem = refs[:-1], refs[-1]
    core, mine, across = here(dev)
    t = dev[0] % 4
    copies = []
    for half in range(2):
        *own, sent = outs[(RING + 1) * half : (RING + 1) * (half + 1)]
        for side in (1, 0):
            first = jnp.where(core == side, t ^ 1, 3 - t)
            second = jnp.where(core == side, 3 - t, t ^ 1)
            for flip in range(RING):
                place = (across if side else mine) ^ flip
                for rank, slab in enumerate((t, second) if half else (first, t ^ 2)):
                    start = pl.multiple_of((2 * slab + place % 2) * BLOCK, TILE)
                    copies.append(
                        pltpu.make_async_copy(
                            act.at[core ^ side, place // 2, :, pl.ds(start, BLOCK)],
                            (sent.at[flip] if side else own[flip]).at[rank],
                            sem.at[len(copies)],
                        )
                    )
                    copies[-1].start()
    for copy in copies:
        copy.wait()


def gram_kernel(dev, *refs):
    ins, outs, tri = refs[: 2 * RING], refs[2 * RING : 3 * RING], refs[3 * RING]
    ins = [*ins[:-1], ins[-1].at[0]]
    across = here(dev)[2]
    for slab in range(2):

        def product(low, high):
            return lax.dot_general(
                jnp.concatenate([ref[slab, :, low:high] for ref in ins]),
                jnp.concatenate([ref[slab, :, low:] for ref in ins]),
                (((0,), (0,)), ((), ())),
                preferred_element_type=jnp.float32,
            )

        top = product(0, 256)
        tri[0:128, :] = top[0:128]
        tri[128:256, 0:512] = top[128:256, 128:]
        middle = product(256, 512)
        tri[256:384, 0:384] = middle[0:128]
        tri[256:384, 384:640] = middle[128:256, 128:]
        tri[128:256, 512:640] = product(512, 640)
        for flip in range(RING):
            start = pl.multiple_of((across ^ flip) * CHUNK, 32)
            outs[flip][slab] = tri[pl.ds(start, CHUNK), :].astype(jnp.bfloat16)


def newton_kernel(tokens_all, dev, newton_steps, *refs):
    ins, (out, total, mixed, gap, mixed_half, gap_half) = refs[:RING], refs[RING:]
    t = dev[0] % 4
    core, place, across = here(dev)
    for flip in range(RING):
        start = pl.multiple_of((across ^ flip) * CHUNK, 32)
        total[pl.ds(start, CHUNK), :] = ins[3 - flip][...]
    steps = newton_steps[core, place // 2, 2 * t + place % 2]
    eye = (
        lax.broadcasted_iota(jnp.int32, (BLOCK, BLOCK), 0)
        == lax.broadcasted_iota(jnp.int32, (BLOCK, BLOCK), 1)
    ).astype(jnp.float32)
    squares = jnp.zeros((TILE, TILE), jnp.float32)
    for i, (row, col) in enumerate(PANELS):
        low = TILE * i
        panel = total[row : row + TILE, col : col + BLOCK - low]
        for j in range(i, 5):
            tile = panel[:, TILE * (j - i) : TILE * (j - i + 1)].astype(jnp.float32)
            tile = tile * (1.0 / tokens_all)
            if i == j:
                tile = tile + DAMPING * eye[:TILE, :TILE]
            mixed[low : low + TILE, TILE * j : TILE * (j + 1)] = tile
            squares = squares + (1.0 if i == j else 2.0) * tile * tile
            if i != j:
                mixed[TILE * j : TILE * (j + 1), low : low + TILE] = tile.T
    norm_scale = jnp.sqrt(jnp.sum(squares))
    scale = 1.0 / norm_scale

    def dot(a, b):
        return jnp.dot(a, b, preferred_element_type=jnp.float32)

    bands = (slice(0, 256), slice(256, 512), slice(512, 640))
    for band in bands:
        start = mixed[band, :] * scale
        gap[band, :] = start
        mixed_half[0, band, :] = start.astype(jnp.bfloat16)
        gap_half[band, :] = start.astype(jnp.bfloat16)
    for band in bands:
        value = 2.0 * gap[band, :] - dot(mixed_half[0, band, :], mixed_half[0])
        mixed[band, :] = value
        mixed_half[1, band, :] = value.astype(jnp.bfloat16)
    for turn in range(1, 3):
        now = turn % 2
        for band in bands:
            old, old_gap = mixed[band, :], gap[band, :]
            new = 2.0 * old - dot(mixed_half[now, band, :], mixed_half[now])
            mixed[band, :] = new
            mixed_half[1 - now, band, :] = new.astype(jnp.bfloat16)
            new_gap = 2.0 * old_gap + 2.0**turn * old - dot(gap_half[band, :], mixed_half[now])
            new_gap = jnp.where(turn < steps, new_gap, old_gap)
            gap[band, :] = new_gap
            gap_half[band, :] = new_gap.astype(jnp.bfloat16)
    reach = jnp.where(steps <= 1, 2.0, jnp.where(steps == 2, 4.0, jnp.where(steps == 3, 8.0, 16.0)))
    for band in bands:
        begin = band.start
        old_gap = gap[band, begin:]
        new_gap = 2.0 * old_gap + 8.0 * mixed[band, begin:]
        new_gap = new_gap - dot(gap_half[band, :], mixed_half[1, :, begin:])
        value = reach * eye[band, begin:] - jnp.where(3 < steps, new_gap, old_gap)
        value = (value * scale).astype(jnp.bfloat16)
        for i in range(begin // TILE, band.stop // TILE):
            row, col = PANELS[i]
            low = TILE * i
            out[row : row + TILE, col : col + BLOCK - low] = value[
                low - begin : low - begin + TILE, low - begin :
            ]


def apply_kernel(side, dev, *refs):
    ins, grads, outs = refs[:RING], refs[RING : RING + 2], refs[-8:-6]
    ins_here, outs_here, whole, sem = refs[-6:-4], refs[-4:-2], refs[-2], refs[-1]
    core, mine, across = here(dev)
    layer = core ^ side
    mine = across if side else mine
    loads = [
        pltpu.make_async_copy(grad.at[layer], place, sem.at[kind])
        for kind, (grad, place) in enumerate(zip(grads, ins_here))
    ]
    stores = [
        pltpu.make_async_copy(place, out.at[layer], sem.at[2 + kind])
        for kind, (out, place) in enumerate(zip(outs, outs_here))
    ]
    for load in loads:
        load.start()

    def unfold(block, place):
        for i, (row, col) in enumerate(PANELS):
            low = TILE * i
            panel = block[row : row + TILE, col : col + BLOCK - low]
            whole[place, low : low + TILE, low:] = panel
            if i % 2 == 0 and i < 4:
                whole[place, low + TILE : low + 2 * TILE, low : low + TILE] = panel[
                    :, TILE : 2 * TILE
                ].T

    def dot(a, b):
        return jnp.dot(a, b, preferred_element_type=jnp.float32)

    def dot_transposed(a, b):
        return lax.dot_general(a, b, (((1,), (1,)), ((), ())), preferred_element_type=jnp.float32)

    for flip in range(RING):
        unfold(ins[flip], mine ^ flip)
    for place in range(RING):
        kind, j = place // 2, place % 2
        if j == 0:
            loads[kind].wait()
        at = j * BLOCK
        rows = ins_here[kind]
        part_0, part_1 = rows[:, at : at + 256], rows[:, at + 256 : at + 512]
        part_2, part_12 = rows[:, at + 512 : at + 640], rows[:, at + 256 : at + 640]
        top = dot(part_0, whole[place, 0:256, :])
        middle = dot(part_1, whole[place, 256:512, 256:])
        low = dot(part_2, whole[place, 512:640, 512:])
        left = top[:, 0:256] + dot_transposed(part_12, whole[place, 0:256, 256:])
        centre = (
            top[:, 256:512]
            + middle[:, 0:256]
            + dot_transposed(part_2, whole[place, 256:512, 512:])
        )
        right = top[:, 512:] + middle[:, 256:] + low
        outs_here[kind][:, at : at + 256] = left.astype(jnp.bfloat16)
        outs_here[kind][:, at + 256 : at + 512] = centre.astype(jnp.bfloat16)
        outs_here[kind][:, at + 512 : at + 640] = right.astype(jnp.bfloat16)
        if j == 1:
            stores[kind].start()
    for store in stores:
        store.wait()


def local(activations, grad_qkv, grad_up, newton_steps):
    half = jnp.bfloat16
    dev = (lax.axis_index("dp") * 4 + lax.axis_index("tensor")).astype(jnp.int32).reshape(1)
    rows = activations.shape[2]
    tokens_all = rows * 256

    def shape(*dims):
        return jax.ShapeDtypeStruct(dims, half)

    def wide(array):
        return array.astype(jnp.float32)

    def over_square(parts, of_places):
        moved = {flip: in_square(parts[flip], flip, of_places) for flip in (3, 2, 1)}
        return [parts[0]] + [moved[flip] for flip in (1, 2, 3)]

    part = (2, rows, BLOCK)
    packed = pl.pallas_call(
        pack_kernel,
        out_shape=([shape(*part)] * RING + [shape(RING, *part)]) * 2,
        in_specs=[SMEM, ANY],
        out_specs=[ANY] * (2 * RING + 2),
        scratch_shapes=[pltpu.SemaphoreType.DMA((4 * RING * 2,))],
        compiler_params=pltpu.CompilerParams(vmem_limit_bytes=48 * 1024 * 1024),
        name="pack",
    )(dev, activations)

    def factors(own, sent):
        received = to_other_core(sent)
        own = over_square(own, True)
        others = [in_square(received[flip], flip, True) for flip in (3, 2, 1)]
        chunks = pl.pallas_call(
            gram_kernel,
            out_shape=[shape(2, CHUNK, BLOCK)] * RING,
            in_specs=[SMEM] + [VMEM] * (2 * RING),
            out_specs=[VMEM] * RING,
            scratch_shapes=[pltpu.VMEM((PACK, BLOCK), jnp.float32)],
            compiler_params=PARAMS,
            name="gram",
        )(dev, *own[::-1], *others, received)
        chunks = over_square(chunks, False)
        return sum(wide(chunk) for chunk in chunks[::-1])

    leaving = to_slab(factors(packed[:RING], packed[RING]).astype(half), 0)
    sums = factors(packed[RING + 1 : -1], packed[-1]) + wide(leaving)
    sums = sums[0] + wide(to_slab(sums[1].astype(half), 1))
    sums = sums + wide(to_z_neighbour(sums.astype(half)))
    members = over_square([sums.astype(half)] * RING, False)

    inverse = pl.pallas_call(
        functools.partial(newton_kernel, tokens_all),
        out_shape=shape(PACK, BLOCK),
        in_specs=[SMEM, SMEM] + [VMEM] * RING,
        out_specs=VMEM,
        scratch_shapes=[
            pltpu.VMEM((PACK, BLOCK), half),
            pltpu.VMEM((BLOCK, BLOCK), jnp.float32),
            pltpu.VMEM((BLOCK, BLOCK), jnp.float32),
            pltpu.VMEM((2, BLOCK, BLOCK), half),
            pltpu.VMEM((BLOCK, BLOCK), half),
        ],
        compiler_params=PARAMS,
        name="newton",
    )(dev, newton_steps, *members[::-1])
    mine = over_square([inverse] * RING, True)
    others = [to_other_core(block) for block in mine]

    def apply(side, blocks, before):
        kinds = (grad_qkv.shape, grad_up.shape)
        buffers = [pltpu.VMEM(dims[1:], half) for dims in kinds]
        return pl.pallas_call(
            functools.partial(apply_kernel, side),
            out_shape=[shape(*dims) for dims in kinds],
            in_specs=[SMEM] + [VMEM] * RING + [ANY] * (2 + len(before)),
            out_specs=[ANY] * 2,
            input_output_aliases={7: 0, 8: 1} if before else {},
            scratch_shapes=buffers
            + buffers
            + [
                pltpu.VMEM((RING, BLOCK, BLOCK), half),
                pltpu.SemaphoreType.DMA((4,)),
            ],
            compiler_params=PARAMS,
            name="apply",
        )(dev, *blocks, grad_qkv, grad_up, *before)

    return tuple(apply(1, others, apply(0, mine, ())))


def solution(mesh):
    placed = (
        P(None, None, ("dp", "tensor"), None),
        P(None, "dp", "tensor"),
        P(None, "dp", "tensor"),
        P(),
    )
    return jax.shard_map(
        local,
        mesh=mesh,
        in_specs=placed,
        out_specs=(P(None, "dp", "tensor"), P(None, "dp", "tensor")),
        check_vma=False,
    )
```

```python
import functools

import jax
import jax.numpy as jnp
from jax import lax
from jax.experimental import pallas as pl
from jax.experimental.pallas import tpu as pltpu
from jax.sharding import PartitionSpec as P

DAMPING = 0.05
BLOCK = 640
TILE = 128
PACK = 384
PANELS = ((0, 0), (128, 0), (256, 0), (256, 384), (128, 512))
RING = 4
SLABS = 4
CHUNK = PACK // RING
AXES = ("dp", "tensor")
PARAMS = pltpu.CompilerParams(vmem_limit_bytes=24 * 1024 * 1024)
SMEM = pl.BlockSpec(memory_space=pltpu.SMEM)
VMEM = pl.BlockSpec(memory_space=pltpu.VMEM)
ANY = pl.BlockSpec(memory_space=pl.ANY)


def bit_a(i):
    return (i + 1) // 2 % 2


def bit_b(i):
    return i // 2


def device_at(device):
    dp, t = device // 4, device % 4
    return dp // 32, dp // 8 % 4, dp // 2 % 4, dp % 2, t


def move(array, target):
    pairs = []
    for device in range(256):
        zl, x, y, c, t = target(*device_at(device))
        pairs.append((device, (((zl * 4 + x) * 4 + y) * 2 + c) * 4 + t))
    return lax.ppermute(array, AXES, pairs)


def to_other_core(array):
    return move(array, lambda zl, x, y, c, t: (zl, x, y, 1 - c, t))


def in_square(array, flip, of_places):
    def target(zl, x, y, c, t):
        x2, y2 = (x ^ 1, y ^ 1) if (c == 0) == of_places else (3 - x, 3 - y)
        return zl, x2 if flip & 2 else x, y2 if flip & 1 else y, c, t

    return move(array, target)


def to_slab(array, step):
    return move(array, lambda zl, x, y, c, t: (zl, x, y, c, 3 - t if c == step else t ^ 1))


def gather_across(array):
    found = {}
    for device in range(256):
        zl, x, y, c, t = device_at(device)
        a, b = 2 * bit_a(x) + bit_a(y), 2 * bit_b(x) + bit_b(y)
        place, across = (a, b) if c == 0 else (b, a)
        found.setdefault((c, zl, t, place), {})[across] = device
    groups = [[found[key][across] for across in range(RING)] for key in sorted(found)]
    array = jnp.broadcast_to(array[None], (RING, *array.shape))
    return lax.all_to_all(array, AXES, 0, 0, axis_index_groups=groups, tiled=True)


def to_z_neighbour(array):
    return move(array, lambda zl, x, y, c, t: (1 - zl, x, y, c, t))


def here(dev):
    dp = dev[0] // 4
    core, x, y = dp % 2, dp // 8 % 4, dp // 2 % 4
    a, b = 2 * bit_a(x) + bit_a(y), 2 * bit_b(x) + bit_b(y)
    return core, jnp.where(core == 0, a, b), jnp.where(core == 0, b, a)


def pack_kernel(dev, act, *refs):
    outs, sem = refs[:-1], refs[-1]
    core, mine, across = here(dev)
    t = dev[0] % 4
    copies = []
    for half in range(2):
        *own, sent = outs[(RING + 1) * half : (RING + 1) * (half + 1)]
        for side in (1, 0):
            first = jnp.where(core == side, 3 - t, t ^ 1)
            second = jnp.where(core == side, t ^ 1, 3 - t)
            for flip in range(RING):
                place = (across if side else mine) ^ flip
                for rank, slab in enumerate((t, second) if half else (first, t ^ 2)):
                    start = pl.multiple_of((2 * slab + place % 2) * BLOCK, TILE)
                    copies.append(
                        pltpu.make_async_copy(
                            act.at[core ^ side, place // 2, :, pl.ds(start, BLOCK)],
                            (sent.at[flip] if side else own[flip]).at[rank],
                            sem.at[len(copies)],
                        )
                    )
                    copies[-1].start()
    for copy in copies:
        copy.wait()


def gram_kernel(dev, *refs):
    ins, outs, tri = refs[: 2 * RING], refs[2 * RING : 3 * RING], refs[3 * RING]
    ins = [*ins[:-1], ins[-1].at[0]]
    across = here(dev)[2]
    for slab in range(2):

        def product(low, high):
            return lax.dot_general(
                jnp.concatenate([ref[slab, :, low:high] for ref in ins]),
                jnp.concatenate([ref[slab, :, low:] for ref in ins]),
                (((0,), (0,)), ((), ())),
                preferred_element_type=jnp.float32,
            )

        top = product(0, 256)
        tri[0:128, :] = top[0:128]
        tri[128:256, 0:512] = top[128:256, 128:]
        middle = product(256, 512)
        tri[256:384, 0:384] = middle[0:128]
        tri[256:384, 384:640] = middle[128:256, 128:]
        tri[128:256, 512:640] = product(512, 640)
        for flip in range(RING):
            start = pl.multiple_of((across ^ flip) * CHUNK, 32)
            outs[flip][slab] = tri[pl.ds(start, CHUNK), :].astype(jnp.bfloat16)


def newton_kernel(
    tokens_all, dev, newton_steps, total, out, mixed, gap, mixed_half, gap_half
):
    t = dev[0] % 4
    core, place, _ = here(dev)
    steps = newton_steps[core, place // 2, 2 * t + place % 2]
    eye = (
        lax.broadcasted_iota(jnp.int32, (BLOCK, BLOCK), 0)
        == lax.broadcasted_iota(jnp.int32, (BLOCK, BLOCK), 1)
    ).astype(jnp.float32)
    squares = jnp.zeros((TILE, TILE), jnp.float32)
    for i, (row, col) in enumerate(PANELS):
        low = TILE * i
        panel = total[row : row + TILE, col : col + BLOCK - low]
        for j in range(i, 5):
            tile = panel[:, TILE * (j - i) : TILE * (j - i + 1)].astype(jnp.float32)
            tile = tile * (1.0 / tokens_all)
            if i == j:
                tile = tile + DAMPING * eye[:TILE, :TILE]
            mixed[low : low + TILE, TILE * j : TILE * (j + 1)] = tile
            squares = squares + (1.0 if i == j else 2.0) * tile * tile
            if i != j:
                mixed[TILE * j : TILE * (j + 1), low : low + TILE] = tile.T
    norm_scale = jnp.sqrt(jnp.sum(squares))
    scale = 1.0 / norm_scale

    def dot(a, b):
        return jnp.dot(a, b, preferred_element_type=jnp.float32)

    bands = (slice(0, 256), slice(256, 512), slice(512, 640))
    for band in bands:
        start = mixed[band, :] * scale
        gap[band, :] = start
        mixed_half[0, band, :] = start.astype(jnp.bfloat16)
        gap_half[band, :] = start.astype(jnp.bfloat16)
    for band in bands:
        value = 2.0 * gap[band, :] - dot(mixed_half[0, band, :], mixed_half[0])
        mixed[band, :] = value
        mixed_half[1, band, :] = value.astype(jnp.bfloat16)
    for turn in range(1, 3):
        now = turn % 2
        for band in bands:
            old, old_gap = mixed[band, :], gap[band, :]
            new = 2.0 * old - dot(mixed_half[now, band, :], mixed_half[now])
            mixed[band, :] = new
            mixed_half[1 - now, band, :] = new.astype(jnp.bfloat16)
            new_gap = 2.0 * old_gap + 2.0**turn * old - dot(gap_half[band, :], mixed_half[now])
            new_gap = jnp.where(turn < steps, new_gap, old_gap)
            gap[band, :] = new_gap
            gap_half[band, :] = new_gap.astype(jnp.bfloat16)
    reach = jnp.where(steps <= 1, 2.0, jnp.where(steps == 2, 4.0, jnp.where(steps == 3, 8.0, 16.0)))
    for band in bands:
        begin = band.start
        old_gap = gap[band, begin:]
        new_gap = 2.0 * old_gap + 8.0 * mixed[band, begin:]
        new_gap = new_gap - dot(gap_half[band, :], mixed_half[1, :, begin:])
        value = reach * eye[band, begin:] - jnp.where(3 < steps, new_gap, old_gap)
        value = (value * scale).astype(jnp.bfloat16)
        for i in range(begin // TILE, band.stop // TILE):
            row, col = PANELS[i]
            low = TILE * i
            out[row : row + TILE, col : col + BLOCK - low] = value[
                low - begin : low - begin + TILE, low - begin :
            ]


def apply_kernel(side, dev, *refs):
    ins, grads, outs = refs[:RING], refs[RING : RING + 2], refs[-6:-4]
    outs_here, whole, sem = refs[-4:-2], refs[-2], refs[-1]
    core, mine, across = here(dev)
    layer = core ^ side
    mine = across if side else mine
    stores = []

    def unfold(block, place):
        for i, (row, col) in enumerate(PANELS):
            low = TILE * i
            panel = block[row : row + TILE, col : col + BLOCK - low]
            whole[place, low : low + TILE, low:] = panel
            if i % 2 == 0 and i < 4:
                whole[place, low + TILE : low + 2 * TILE, low : low + TILE] = panel[
                    :, TILE : 2 * TILE
                ].T

    def dot(a, b):
        return jnp.dot(a, b, preferred_element_type=jnp.float32)

    def dot_transposed(a, b):
        return lax.dot_general(a, b, (((1,), (1,)), ((), ())), preferred_element_type=jnp.float32)

    for flip in range(RING):
        unfold(ins[flip], mine ^ flip)
    for place in range(RING):
        kind, j = place // 2, place % 2
        at = j * BLOCK

        def columns(start, stop):
            return grads[kind][layer, :, at + start : at + stop]

        part_0, part_1 = columns(0, 256), columns(256, 512)
        part_2, part_12 = columns(512, 640), columns(256, 640)
        top = dot(part_0, whole[place, 0:256, :])
        middle = dot(part_1, whole[place, 256:512, 256:])
        low = dot(part_2, whole[place, 512:640, 512:])
        left = top[:, 0:256] + dot_transposed(part_12, whole[place, 0:256, 256:])
        centre = (
            top[:, 256:512]
            + middle[:, 0:256]
            + dot_transposed(part_2, whole[place, 256:512, 512:])
        )
        right = top[:, 512:] + middle[:, 256:] + low
        outs_here[kind][:, at : at + 256] = left.astype(jnp.bfloat16)
        outs_here[kind][:, at + 256 : at + 512] = centre.astype(jnp.bfloat16)
        outs_here[kind][:, at + 512 : at + 640] = right.astype(jnp.bfloat16)
        done = pl.ds(at, BLOCK)
        stores.append(
            pltpu.make_async_copy(
                outs_here[kind].at[:, done], outs[kind].at[layer, :, done], sem.at[place]
            )
        )
        stores[-1].start()
    for store in stores:
        store.wait()


def local(activations, grad_qkv, grad_up, newton_steps):
    half = jnp.bfloat16
    dev = (lax.axis_index("dp") * 4 + lax.axis_index("tensor")).astype(jnp.int32).reshape(1)
    rows = activations.shape[2]
    tokens_all = rows * 256

    def shape(*dims):
        return jax.ShapeDtypeStruct(dims, half)

    def wide(array):
        return array.astype(jnp.float32)

    def over_square(parts, of_places):
        moved = {flip: in_square(parts[flip], flip, of_places) for flip in (3, 2, 1)}
        return [parts[0]] + [moved[flip] for flip in (1, 2, 3)]

    part = (2, rows, BLOCK)
    packed = pl.pallas_call(
        pack_kernel,
        out_shape=([shape(*part)] * RING + [shape(RING, *part)]) * 2,
        in_specs=[SMEM, ANY],
        out_specs=[ANY] * (2 * RING + 2),
        scratch_shapes=[pltpu.SemaphoreType.DMA((4 * RING * 2,))],
        compiler_params=pltpu.CompilerParams(vmem_limit_bytes=48 * 1024 * 1024),
        name="pack",
    )(dev, activations)

    def factors(own, sent):
        received = to_other_core(sent)
        own = over_square(own, True)
        others = [in_square(received[flip], flip, True) for flip in (3, 2, 1)]
        chunks = pl.pallas_call(
            gram_kernel,
            out_shape=[shape(2, CHUNK, BLOCK)] * RING,
            in_specs=[SMEM] + [VMEM] * (2 * RING),
            out_specs=[VMEM] * RING,
            scratch_shapes=[pltpu.VMEM((PACK, BLOCK), jnp.float32)],
            compiler_params=PARAMS,
            name="gram",
        )(dev, *own[::-1], *others, received)
        chunks = over_square(chunks, False)
        return sum(wide(chunk) for chunk in chunks[::-1])

    leaving = to_slab(factors(packed[:RING], packed[RING]).astype(half), 0)
    sums = factors(packed[RING + 1 : -1], packed[-1]) + wide(leaving)
    sums = sums[0] + wide(to_slab(sums[1].astype(half), 1))
    sums = sums + wide(to_z_neighbour(sums.astype(half)))
    total = gather_across(sums.astype(half)).reshape(PACK, BLOCK)

    inverse = pl.pallas_call(
        functools.partial(newton_kernel, tokens_all),
        out_shape=shape(PACK, BLOCK),
        in_specs=[SMEM, SMEM, VMEM],
        out_specs=VMEM,
        scratch_shapes=[
            pltpu.VMEM((BLOCK, BLOCK), jnp.float32),
            pltpu.VMEM((BLOCK, BLOCK), jnp.float32),
            pltpu.VMEM((2, BLOCK, BLOCK), half),
            pltpu.VMEM((BLOCK, BLOCK), half),
        ],
        compiler_params=PARAMS,
        name="newton",
    )(dev, newton_steps, total)
    mine = over_square([inverse] * RING, True)
    others = [to_other_core(block) for block in mine]

    def apply(side, blocks, before):
        kinds = (grad_qkv.shape, grad_up.shape)
        buffers = [pltpu.VMEM(dims[1:], half) for dims in kinds]
        return pl.pallas_call(
            functools.partial(apply_kernel, side),
            out_shape=[shape(*dims) for dims in kinds],
            in_specs=[SMEM] + [VMEM] * (RING + 2) + [ANY] * len(before),
            out_specs=[ANY] * 2,
            input_output_aliases={7: 0, 8: 1} if before else {},
            scratch_shapes=buffers
            + [
                pltpu.VMEM((RING, BLOCK, BLOCK), half),
                pltpu.SemaphoreType.DMA((4,)),
            ],
            compiler_params=PARAMS,
            name="apply",
        )(dev, *blocks, grad_qkv, grad_up, *before)

    return tuple(apply(1, others, apply(0, mine, ())))


def solution(mesh):
    placed = (
        P(None, None, ("dp", "tensor"), None),
        P(None, "dp", "tensor"),
        P(None, "dp", "tensor"),
        P(),
    )
    return jax.shard_map(
        local,
        mesh=mesh,
        in_specs=placed,
        out_specs=(P(None, "dp", "tensor"), P(None, "dp", "tensor")),
        check_vma=False,
    )
```

```python
import functools

import jax
import jax.numpy as jnp
from jax import lax
from jax.experimental import pallas as pl
from jax.experimental.pallas import tpu as pltpu
from jax.sharding import PartitionSpec as P

DAMPING = 0.05
BLOCK = 640
TILE = 128
PACK = 384
PANELS = ((0, 0), (128, 0), (256, 0), (256, 384), (128, 512))
RING = 4
SLABS = 4
CHUNK = PACK // RING
AXES = ("dp", "tensor")
PARAMS = pltpu.CompilerParams(vmem_limit_bytes=24 * 1024 * 1024)
SMEM = pl.BlockSpec(memory_space=pltpu.SMEM)
VMEM = pl.BlockSpec(memory_space=pltpu.VMEM)
ANY = pl.BlockSpec(memory_space=pl.ANY)


def bit_a(i):
    return (i + 1) // 2 % 2


def bit_b(i):
    return i // 2


def device_at(device):
    dp, t = device // 4, device % 4
    return dp // 32, dp // 8 % 4, dp // 2 % 4, dp % 2, t


def move(array, target):
    pairs = []
    for device in range(256):
        zl, x, y, c, t = target(*device_at(device))
        pairs.append((device, (((zl * 4 + x) * 4 + y) * 2 + c) * 4 + t))
    return lax.ppermute(array, AXES, pairs)


def to_other_core(array):
    return move(array, lambda zl, x, y, c, t: (zl, x, y, 1 - c, t))


def in_square(array, flip, of_places):
    def target(zl, x, y, c, t):
        x2, y2 = (x ^ 1, 3 - y) if (c == 0) == of_places else (3 - x, y ^ 1)
        return zl, x2 if flip & 2 else x, y2 if flip & 1 else y, c, t

    return move(array, target)


def to_slab(array, step):
    return move(array, lambda zl, x, y, c, t: (zl, x, y, c, t ^ 1 if c == step else 3 - t))


def to_z_neighbour(array):
    return move(array, lambda zl, x, y, c, t: (1 - zl, x, y, c, t))


def here(dev):
    dp = dev[0] // 4
    core, x, y = dp % 2, dp // 8 % 4, dp // 2 % 4
    a, b = 2 * bit_a(x) + bit_b(y), 2 * bit_b(x) + bit_a(y)
    return core, jnp.where(core == 0, a, b), jnp.where(core == 0, b, a)


def pack_kernel(dev, act, *refs):
    outs, sem = refs[:-1], refs[-1]
    core, mine, across = here(dev)
    t = dev[0] % 4
    copies = []
    for half in range(2):
        *own, sent = outs[(RING + 1) * half : (RING + 1) * (half + 1)]
        for side in (1, 0):
            first = jnp.where(core == side, t ^ 1, 3 - t)
            second = jnp.where(core == side, 3 - t, t ^ 1)
            for flip in range(RING):
                place = (across if side else mine) ^ flip
                for rank, slab in enumerate((t, second) if half else (first, t ^ 2)):
                    start = pl.multiple_of((2 * slab + place % 2) * BLOCK, TILE)
                    copies.append(
                        pltpu.make_async_copy(
                            act.at[core ^ side, place // 2, :, pl.ds(start, BLOCK)],
                            (sent.at[flip] if side else own[flip]).at[rank],
                            sem.at[len(copies)],
                        )
                    )
                    copies[-1].start()
    for copy in copies:
        copy.wait()


def gram_kernel(dev, *refs):
    ins, outs, tri = refs[: 2 * RING], refs[2 * RING : 3 * RING], refs[3 * RING]
    ins = [*ins[:-1], ins[-1].at[0]]
    across = here(dev)[2]
    for slab in range(2):

        def product(low, high):
            return lax.dot_general(
                jnp.concatenate([ref[slab, :, low:high] for ref in ins]),
                jnp.concatenate([ref[slab, :, low:] for ref in ins]),
                (((0,), (0,)), ((), ())),
                preferred_element_type=jnp.float32,
            )

        top = product(0, 256)
        tri[0:128, :] = top[0:128]
        tri[128:256, 0:512] = top[128:256, 128:]
        middle = product(256, 512)
        tri[256:384, 0:384] = middle[0:128]
        tri[256:384, 384:640] = middle[128:256, 128:]
        tri[128:256, 512:640] = product(512, 640)
        for flip in range(RING):
            start = pl.multiple_of((across ^ flip) * CHUNK, 32)
            outs[flip][slab] = tri[pl.ds(start, CHUNK), :].astype(jnp.bfloat16)


def newton_kernel(tokens_all, dev, newton_steps, *refs):
    ins, (out, total, mixed, gap, mixed_half, gap_half) = refs[:RING], refs[RING:]
    t = dev[0] % 4
    core, place, across = here(dev)
    for flip in range(RING):
        start = pl.multiple_of((across ^ flip) * CHUNK, 32)
        total[pl.ds(start, CHUNK), :] = ins[3 - flip][...]
    steps = newton_steps[core, place // 2, 2 * t + place % 2]
    eye = (
        lax.broadcasted_iota(jnp.int32, (BLOCK, BLOCK), 0)
        == lax.broadcasted_iota(jnp.int32, (BLOCK, BLOCK), 1)
    ).astype(jnp.float32)
    squares = jnp.zeros((TILE, TILE), jnp.float32)
    for i, (row, col) in enumerate(PANELS):
        low = TILE * i
        panel = total[row : row + TILE, col : col + BLOCK - low]
        for j in range(i, 5):
            tile = panel[:, TILE * (j - i) : TILE * (j - i + 1)].astype(jnp.float32)
            tile = tile * (1.0 / tokens_all)
            if i == j:
                tile = tile + DAMPING * eye[:TILE, :TILE]
            mixed[low : low + TILE, TILE * j : TILE * (j + 1)] = tile
            squares = squares + (1.0 if i == j else 2.0) * tile * tile
            if i != j:
                mixed[TILE * j : TILE * (j + 1), low : low + TILE] = tile.T
    norm_scale = jnp.sqrt(jnp.sum(squares))
    scale = 1.0 / norm_scale

    def dot(a, b):
        return jnp.dot(a, b, preferred_element_type=jnp.float32)

    bands = (slice(0, 256), slice(256, 512), slice(512, 640))
    for band in bands:
        start = mixed[band, :] * scale
        gap[band, :] = start
        mixed_half[0, band, :] = start.astype(jnp.bfloat16)
        gap_half[band, :] = start.astype(jnp.bfloat16)
    for band in bands:
        value = 2.0 * gap[band, :] - dot(mixed_half[0, band, :], mixed_half[0])
        mixed[band, :] = value
        mixed_half[1, band, :] = value.astype(jnp.bfloat16)
    for turn in range(1, 3):
        now = turn % 2
        for band in bands:
            old, old_gap = mixed[band, :], gap[band, :]
            new = 2.0 * old - dot(mixed_half[now, band, :], mixed_half[now])
            mixed[band, :] = new
            mixed_half[1 - now, band, :] = new.astype(jnp.bfloat16)
            new_gap = 2.0 * old_gap + 2.0**turn * old - dot(gap_half[band, :], mixed_half[now])
            new_gap = jnp.where(turn < steps, new_gap, old_gap)
            gap[band, :] = new_gap
            gap_half[band, :] = new_gap.astype(jnp.bfloat16)
    reach = jnp.where(steps <= 1, 2.0, jnp.where(steps == 2, 4.0, jnp.where(steps == 3, 8.0, 16.0)))
    for band in bands:
        begin = band.start
        old_gap = gap[band, begin:]
        new_gap = 2.0 * old_gap + 8.0 * mixed[band, begin:]
        new_gap = new_gap - dot(gap_half[band, :], mixed_half[1, :, begin:])
        value = reach * eye[band, begin:] - jnp.where(3 < steps, new_gap, old_gap)
        value = (value * scale).astype(jnp.bfloat16)
        for i in range(begin // TILE, band.stop // TILE):
            row, col = PANELS[i]
            low = TILE * i
            out[row : row + TILE, col : col + BLOCK - low] = value[
                low - begin : low - begin + TILE, low - begin :
            ]


def apply_kernel(side, dev, *refs):
    ins, grads, outs = refs[:RING], refs[RING : RING + 2], refs[-6:-4]
    outs_here, whole, sem = refs[-4:-2], refs[-2], refs[-1]
    core, mine, across = here(dev)
    layer = core ^ side
    mine = across if side else mine
    stores = []

    def unfold(block, place):
        for i, (row, col) in enumerate(PANELS):
            low = TILE * i
            panel = block[row : row + TILE, col : col + BLOCK - low]
            whole[place, low : low + TILE, low:] = panel
            if i % 2 == 0 and i < 4:
                whole[place, low + TILE : low + 2 * TILE, low : low + TILE] = panel[
                    :, TILE : 2 * TILE
                ].T

    def dot(a, b):
        return jnp.dot(a, b, preferred_element_type=jnp.float32)

    def dot_transposed(a, b):
        return lax.dot_general(a, b, (((1,), (1,)), ((), ())), preferred_element_type=jnp.float32)

    for flip in range(RING):
        unfold(ins[flip], mine ^ flip)
    for place in range(RING):
        kind, j = place // 2, place % 2
        at = j * BLOCK

        def columns(start, stop):
            return grads[kind][layer, :, at + start : at + stop]

        part_0, part_1 = columns(0, 256), columns(256, 512)
        part_2, part_12 = columns(512, 640), columns(256, 640)
        top = dot(part_0, whole[place, 0:256, :])
        middle = dot(part_1, whole[place, 256:512, 256:])
        low = dot(part_2, whole[place, 512:640, 512:])
        left = top[:, 0:256] + dot_transposed(part_12, whole[place, 0:256, 256:])
        centre = (
            top[:, 256:512]
            + middle[:, 0:256]
            + dot_transposed(part_2, whole[place, 256:512, 512:])
        )
        right = top[:, 512:] + middle[:, 256:] + low
        outs_here[kind][:, at : at + 256] = left.astype(jnp.bfloat16)
        outs_here[kind][:, at + 256 : at + 512] = centre.astype(jnp.bfloat16)
        outs_here[kind][:, at + 512 : at + 640] = right.astype(jnp.bfloat16)
        done = pl.ds(at, BLOCK)
        stores.append(
            pltpu.make_async_copy(
                outs_here[kind].at[:, done], outs[kind].at[layer, :, done], sem.at[place]
            )
        )
        stores[-1].start()
    for store in stores:
        store.wait()


def local(activations, grad_qkv, grad_up, newton_steps):
    half = jnp.bfloat16
    dev = (lax.axis_index("dp") * 4 + lax.axis_index("tensor")).astype(jnp.int32).reshape(1)
    rows = activations.shape[2]
    tokens_all = rows * 256

    def shape(*dims):
        return jax.ShapeDtypeStruct(dims, half)

    def wide(array):
        return array.astype(jnp.float32)

    def over_square(parts, of_places):
        moved = {flip: in_square(parts[flip], flip, of_places) for flip in (3, 2, 1)}
        return [parts[0]] + [moved[flip] for flip in (1, 2, 3)]

    part = (2, rows, BLOCK)
    packed = pl.pallas_call(
        pack_kernel,
        out_shape=([shape(*part)] * RING + [shape(RING, *part)]) * 2,
        in_specs=[SMEM, ANY],
        out_specs=[ANY] * (2 * RING + 2),
        scratch_shapes=[pltpu.SemaphoreType.DMA((4 * RING * 2,))],
        compiler_params=pltpu.CompilerParams(vmem_limit_bytes=48 * 1024 * 1024),
        name="pack",
    )(dev, activations)

    def factors(own, sent):
        received = to_other_core(sent)
        own = over_square(own, True)
        others = [in_square(received[flip], flip, True) for flip in (3, 2, 1)]
        chunks = pl.pallas_call(
            gram_kernel,
            out_shape=[shape(2, CHUNK, BLOCK)] * RING,
            in_specs=[SMEM] + [VMEM] * (2 * RING),
            out_specs=[VMEM] * RING,
            scratch_shapes=[pltpu.VMEM((PACK, BLOCK), jnp.float32)],
            compiler_params=PARAMS,
            name="gram",
        )(dev, *own[::-1], *others, received)
        chunks = over_square(chunks, False)
        return sum(wide(chunk) for chunk in chunks[::-1])

    leaving = to_slab(factors(packed[:RING], packed[RING]).astype(half), 0)
    sums = factors(packed[RING + 1 : -1], packed[-1]) + wide(leaving)
    sums = sums[0] + wide(to_slab(sums[1].astype(half), 1))
    sums = sums + wide(to_z_neighbour(sums.astype(half)))
    members = over_square([sums.astype(half)] * RING, False)

    inverse = pl.pallas_call(
        functools.partial(newton_kernel, tokens_all),
        out_shape=shape(PACK, BLOCK),
        in_specs=[SMEM, SMEM] + [VMEM] * RING,
        out_specs=VMEM,
        scratch_shapes=[
            pltpu.VMEM((PACK, BLOCK), half),
            pltpu.VMEM((BLOCK, BLOCK), jnp.float32),
            pltpu.VMEM((BLOCK, BLOCK), jnp.float32),
            pltpu.VMEM((2, BLOCK, BLOCK), half),
            pltpu.VMEM((BLOCK, BLOCK), half),
        ],
        compiler_params=PARAMS,
        name="newton",
    )(dev, newton_steps, *members[::-1])
    mine = over_square([inverse] * RING, True)
    others = [to_other_core(block) for block in mine]

    def apply(side, blocks, before):
        kinds = (grad_qkv.shape, grad_up.shape)
        buffers = [pltpu.VMEM(dims[1:], half) for dims in kinds]
        return pl.pallas_call(
            functools.partial(apply_kernel, side),
            out_shape=[shape(*dims) for dims in kinds],
            in_specs=[SMEM] + [VMEM] * (RING + 2) + [ANY] * len(before),
            out_specs=[ANY] * 2,
            input_output_aliases={7: 0, 8: 1} if before else {},
            scratch_shapes=buffers
            + [
                pltpu.VMEM((RING, BLOCK, BLOCK), half),
                pltpu.SemaphoreType.DMA((4,)),
            ],
            compiler_params=PARAMS,
            name="apply",
        )(dev, *blocks, grad_qkv, grad_up, *before)

    return tuple(apply(1, others, apply(0, mine, ())))


def solution(mesh):
    placed = (
        P(None, None, ("dp", "tensor"), None),
        P(None, "dp", "tensor"),
        P(None, "dp", "tensor"),
        P(),
    )
    return jax.shard_map(
        local,
        mesh=mesh,
        in_specs=placed,
        out_specs=(P(None, "dp", "tensor"), P(None, "dp", "tensor")),
        check_vma=False,
    )
```

```python
import functools

import jax
import jax.numpy as jnp
from jax import lax
from jax.experimental import pallas as pl
from jax.experimental.pallas import tpu as pltpu
from jax.sharding import PartitionSpec as P

DAMPING = 0.05
BLOCK = 640
TILE = 128
PACK = 384
PANELS = ((0, 0), (128, 0), (256, 0), (256, 384), (128, 512))
RING = 4
SLABS = 4
CHUNK = PACK // RING
AXES = ("dp", "tensor")
PARAMS = pltpu.CompilerParams(vmem_limit_bytes=24 * 1024 * 1024)
SMEM = pl.BlockSpec(memory_space=pltpu.SMEM)
VMEM = pl.BlockSpec(memory_space=pltpu.VMEM)
ANY = pl.BlockSpec(memory_space=pl.ANY)


def bit_a(i):
    return (i + 1) // 2 % 2


def bit_b(i):
    return i // 2


def device_at(device):
    dp, t = device // 4, device % 4
    return dp // 32, dp // 8 % 4, dp // 2 % 4, dp % 2, t


def move(array, target):
    pairs = []
    for device in range(256):
        zl, x, y, c, t = target(*device_at(device))
        pairs.append((device, (((zl * 4 + x) * 4 + y) * 2 + c) * 4 + t))
    return lax.ppermute(array, AXES, pairs)


def to_other_core(array):
    return move(array, lambda zl, x, y, c, t: (zl, x, y, 1 - c, t))


def in_square(array, flip, of_places):
    def target(zl, x, y, c, t):
        x2, y2 = (x ^ 1, y ^ 1) if (c == 0) == of_places else (3 - x, 3 - y)
        return zl, x2 if flip & 2 else x, y2 if flip & 1 else y, c, t

    return move(array, target)


def to_slab(array, step):
    return move(array, lambda zl, x, y, c, t: (zl, x, y, c, t ^ 1 if c == step else 3 - t))


def to_z_neighbour(array):
    return move(array, lambda zl, x, y, c, t: (1 - zl, x, y, c, t))


def here(dev):
    dp = dev[0] // 4
    core, x, y = dp % 2, dp // 8 % 4, dp // 2 % 4
    a, b = 2 * bit_a(x) + bit_a(y), 2 * bit_b(x) + bit_b(y)
    return core, jnp.where(core == 0, a, b), jnp.where(core == 0, b, a)


def pack_kernel(dev, act, *refs):
    outs, sem = refs[:-1], refs[-1]
    core, mine, across = here(dev)
    t = dev[0] % 4
    copies = []
    for half in range(2):
        *own, sent = outs[(RING + 1) * half : (RING + 1) * (half + 1)]
        for side in (1, 0):
            first = jnp.where(core == side, t ^ 1, 3 - t)
            second = jnp.where(core == side, 3 - t, t ^ 1)
            for flip in range(RING):
                place = (across if side else mine) ^ flip
                for rank, slab in enumerate((t, second) if half else (first, t ^ 2)):
                    start = pl.multiple_of((2 * slab + place % 2) * BLOCK, TILE)
                    copies.append(
                        pltpu.make_async_copy(
                            act.at[core ^ side, place // 2, :, pl.ds(start, BLOCK)],
                            (sent.at[flip] if side else own[flip]).at[rank],
                            sem.at[len(copies)],
                        )
                    )
                    copies[-1].start()
    for copy in copies:
        copy.wait()


def gram_kernel(dev, *refs):
    ins, outs, tri = refs[: 2 * RING], refs[2 * RING : 3 * RING], refs[3 * RING]
    ins = [*ins[:-1], ins[-1].at[0]]
    across = here(dev)[2]
    for slab in range(2):

        def product(low, high):
            return lax.dot_general(
                jnp.concatenate([ref[slab, :, low:high] for ref in ins]),
                jnp.concatenate([ref[slab, :, low:] for ref in ins]),
                (((0,), (0,)), ((), ())),
                preferred_element_type=jnp.float32,
            )

        top = product(0, 256)
        tri[0:128, :] = top[0:128]
        tri[128:256, 0:512] = top[128:256, 128:]
        middle = product(256, 512)
        tri[256:384, 0:384] = middle[0:128]
        tri[256:384, 384:640] = middle[128:256, 128:]
        tri[128:256, 512:640] = product(512, 640)
        for flip in range(RING):
            start = pl.multiple_of((across ^ flip) * CHUNK, 32)
            outs[flip][slab] = tri[pl.ds(start, CHUNK), :].astype(jnp.bfloat16)


def newton_kernel(tokens_all, dev, newton_steps, *refs):
    ins, (out, total, mixed, gap, mixed_half, gap_half) = refs[:RING], refs[RING:]
    t = dev[0] % 4
    core, place, across = here(dev)
    for flip in range(RING):
        start = pl.multiple_of((across ^ flip) * CHUNK, 32)
        total[pl.ds(start, CHUNK), :] = ins[3 - flip][...]
    steps = newton_steps[core, place // 2, 2 * t + place % 2]
    eye = (
        lax.broadcasted_iota(jnp.int32, (BLOCK, BLOCK), 0)
        == lax.broadcasted_iota(jnp.int32, (BLOCK, BLOCK), 1)
    ).astype(jnp.float32)
    squares = jnp.zeros((TILE, TILE), jnp.float32)
    for i, (row, col) in enumerate(PANELS):
        low = TILE * i
        panel = total[row : row + TILE, col : col + BLOCK - low]
        for j in range(i, 5):
            tile = panel[:, TILE * (j - i) : TILE * (j - i + 1)].astype(jnp.float32)
            tile = tile * (1.0 / tokens_all)
            if i == j:
                tile = tile + DAMPING * eye[:TILE, :TILE]
            mixed[low : low + TILE, TILE * j : TILE * (j + 1)] = tile
            squares = squares + (1.0 if i == j else 2.0) * tile * tile
            if (i, j) in ((0, 1), (2, 3)):
                mixed[TILE * j : TILE * (j + 1), low : low + TILE] = tile.T
    norm_scale = jnp.sqrt(jnp.sum(squares))
    scale = 1.0 / norm_scale

    def dot(a, b):
        return jnp.dot(a, b, preferred_element_type=jnp.float32)

    bands = (slice(0, 256), slice(256, 512), slice(512, 640))

    def keep(whole, band, value):
        value = value.astype(jnp.bfloat16)
        whole[band, band.start :] = value
        if band.stop < BLOCK:
            whole[band.stop :, band] = value[:, band.stop - band.start :].T

    for band in bands:
        start = mixed[band, band.start :] * scale
        gap[band, band.start :] = start
        keep(mixed_half.at[0], band, start)
        keep(gap_half.at[1], band, start)
    for band in bands:
        right = slice(band.start, BLOCK)
        value = 2.0 * gap[band, right] - dot(mixed_half[0, band, :], mixed_half[0, :, right])
        mixed[band, right] = value
        keep(mixed_half.at[1], band, value)
    for turn in range(1, 3):
        now = turn % 2
        for band in bands:
            right = slice(band.start, BLOCK)
            old, old_gap, operand = mixed[band, right], gap[band, right], mixed_half[now, :, right]
            new = 2.0 * old - dot(mixed_half[now, band, :], operand)
            mixed[band, right] = new
            keep(mixed_half.at[1 - now], band, new)
            new_gap = 2.0 * old_gap + 2.0**turn * old - dot(gap_half[now, band, :], operand)
            new_gap = jnp.where(turn < steps, new_gap, old_gap)
            gap[band, right] = new_gap
            keep(gap_half.at[1 - now], band, new_gap)
    reach = jnp.where(steps <= 1, 2.0, jnp.where(steps == 2, 4.0, jnp.where(steps == 3, 8.0, 16.0)))
    for band in bands:
        begin = band.start
        old_gap = gap[band, begin:]
        new_gap = 2.0 * old_gap + 8.0 * mixed[band, begin:]
        new_gap = new_gap - dot(gap_half[1, band, :], mixed_half[1, :, begin:])
        value = reach * eye[band, begin:] - jnp.where(3 < steps, new_gap, old_gap)
        value = (value * scale).astype(jnp.bfloat16)
        for i in range(begin // TILE, band.stop // TILE):
            row, col = PANELS[i]
            low = TILE * i
            out[row : row + TILE, col : col + BLOCK - low] = value[
                low - begin : low - begin + TILE, low - begin :
            ]


def apply_kernel(side, dev, *refs):
    ins, grads, outs = refs[:RING], refs[RING : RING + 2], refs[-6:-4]
    outs_here, whole, sem = refs[-4:-2], refs[-2], refs[-1]
    core, mine, across = here(dev)
    layer = core ^ side
    mine = across if side else mine
    stores = []

    def unfold(block, place):
        for i, (row, col) in enumerate(PANELS):
            low = TILE * i
            panel = block[row : row + TILE, col : col + BLOCK - low]
            whole[place, low : low + TILE, low:] = panel
            if i % 2 == 0 and i < 4:
                whole[place, low + TILE : low + 2 * TILE, low : low + TILE] = panel[
                    :, TILE : 2 * TILE
                ].T

    def dot(a, b):
        return jnp.dot(a, b, preferred_element_type=jnp.float32)

    def dot_transposed(a, b):
        return lax.dot_general(a, b, (((1,), (1,)), ((), ())), preferred_element_type=jnp.float32)

    for flip in range(RING):
        unfold(ins[flip], mine ^ flip)
    for place in range(RING):
        kind, j = place // 2, place % 2
        at = j * BLOCK

        def columns(start, stop):
            return grads[kind][layer, :, at + start : at + stop]

        part_0, part_1 = columns(0, 256), columns(256, 512)
        part_2, part_12 = columns(512, 640), columns(256, 640)
        top = dot(part_0, whole[place, 0:256, :])
        middle = dot(part_1, whole[place, 256:512, 256:])
        low = dot(part_2, whole[place, 512:640, 512:])
        left = top[:, 0:256] + dot_transposed(part_12, whole[place, 0:256, 256:])
        centre = (
            top[:, 256:512]
            + middle[:, 0:256]
            + dot_transposed(part_2, whole[place, 256:512, 512:])
        )
        right = top[:, 512:] + middle[:, 256:] + low
        outs_here[kind][:, at : at + 256] = left.astype(jnp.bfloat16)
        outs_here[kind][:, at + 256 : at + 512] = centre.astype(jnp.bfloat16)
        outs_here[kind][:, at + 512 : at + 640] = right.astype(jnp.bfloat16)
        done = pl.ds(at, BLOCK)
        stores.append(
            pltpu.make_async_copy(
                outs_here[kind].at[:, done], outs[kind].at[layer, :, done], sem.at[place]
            )
        )
        stores[-1].start()
    for store in stores:
        store.wait()


def local(activations, grad_qkv, grad_up, newton_steps):
    half = jnp.bfloat16
    dev = (lax.axis_index("dp") * 4 + lax.axis_index("tensor")).astype(jnp.int32).reshape(1)
    rows = activations.shape[2]
    tokens_all = rows * 256

    def shape(*dims):
        return jax.ShapeDtypeStruct(dims, half)

    def wide(array):
        return array.astype(jnp.float32)

    def over_square(parts, of_places):
        moved = {flip: in_square(parts[flip], flip, of_places) for flip in (3, 2, 1)}
        return [parts[0]] + [moved[flip] for flip in (1, 2, 3)]

    part = (2, rows, BLOCK)
    packed = pl.pallas_call(
        pack_kernel,
        out_shape=([shape(*part)] * RING + [shape(RING, *part)]) * 2,
        in_specs=[SMEM, ANY],
        out_specs=[ANY] * (2 * RING + 2),
        scratch_shapes=[pltpu.SemaphoreType.DMA((4 * RING * 2,))],
        compiler_params=pltpu.CompilerParams(vmem_limit_bytes=48 * 1024 * 1024),
        name="pack",
    )(dev, activations)

    def factors(own, sent):
        received = to_other_core(sent)
        own = over_square(own, True)
        others = [in_square(received[flip], flip, True) for flip in (3, 2, 1)]
        chunks = pl.pallas_call(
            gram_kernel,
            out_shape=[shape(2, CHUNK, BLOCK)] * RING,
            in_specs=[SMEM] + [VMEM] * (2 * RING),
            out_specs=[VMEM] * RING,
            scratch_shapes=[pltpu.VMEM((PACK, BLOCK), jnp.float32)],
            compiler_params=PARAMS,
            name="gram",
        )(dev, *own[::-1], *others, received)
        chunks = over_square(chunks, False)
        return sum(wide(chunk) for chunk in chunks[::-1])

    leaving = to_slab(factors(packed[:RING], packed[RING]).astype(half), 0)
    sums = factors(packed[RING + 1 : -1], packed[-1]) + wide(leaving)
    sums = sums[0] + wide(to_slab(sums[1].astype(half), 1))
    sums = sums + wide(to_z_neighbour(sums.astype(half)))
    members = over_square([sums.astype(half)] * RING, False)

    inverse = pl.pallas_call(
        functools.partial(newton_kernel, tokens_all),
        out_shape=shape(PACK, BLOCK),
        in_specs=[SMEM, SMEM] + [VMEM] * RING,
        out_specs=VMEM,
        scratch_shapes=[
            pltpu.VMEM((PACK, BLOCK), half),
            pltpu.VMEM((BLOCK, BLOCK), jnp.float32),
            pltpu.VMEM((BLOCK, BLOCK), jnp.float32),
            pltpu.VMEM((2, BLOCK, BLOCK), half),
            pltpu.VMEM((2, BLOCK, BLOCK), half),
        ],
        compiler_params=PARAMS,
        name="newton",
    )(dev, newton_steps, *members[::-1])
    mine = over_square([inverse] * RING, True)
    others = [to_other_core(block) for block in mine]

    def apply(side, blocks, before):
        kinds = (grad_qkv.shape, grad_up.shape)
        buffers = [pltpu.VMEM(dims[1:], half) for dims in kinds]
        return pl.pallas_call(
            functools.partial(apply_kernel, side),
            out_shape=[shape(*dims) for dims in kinds],
            in_specs=[SMEM] + [VMEM] * (RING + 2) + [ANY] * len(before),
            out_specs=[ANY] * 2,
            input_output_aliases={7: 0, 8: 1} if before else {},
            scratch_shapes=buffers
            + [
                pltpu.VMEM((RING, BLOCK, BLOCK), half),
                pltpu.SemaphoreType.DMA((4,)),
            ],
            compiler_params=PARAMS,
            name="apply",
        )(dev, *blocks, grad_qkv, grad_up, *before)

    return tuple(apply(1, others, apply(0, mine, ())))


def solution(mesh):
    placed = (
        P(None, None, ("dp", "tensor"), None),
        P(None, "dp", "tensor"),
        P(None, "dp", "tensor"),
        P(),
    )
    return jax.shard_map(
        local,
        mesh=mesh,
        in_specs=placed,
        out_specs=(P(None, "dp", "tensor"), P(None, "dp", "tensor")),
        check_vma=False,
    )
```

```python
import functools

import jax
import jax.numpy as jnp
from jax import lax
from jax.experimental import pallas as pl
from jax.experimental.pallas import tpu as pltpu
from jax.sharding import PartitionSpec as P

DAMPING = 0.05
BLOCK = 640
TILE = 128
PACK = 384
PANELS = ((0, 0), (128, 0), (256, 0), (256, 384), (128, 512))
RING = 4
SLABS = 4
CHUNK = PACK // RING
AXES = ("dp", "tensor")
PARAMS = pltpu.CompilerParams(vmem_limit_bytes=24 * 1024 * 1024)
SMEM = pl.BlockSpec(memory_space=pltpu.SMEM)
VMEM = pl.BlockSpec(memory_space=pltpu.VMEM)
ANY = pl.BlockSpec(memory_space=pl.ANY)


def bit_a(i):
    return (i + 1) // 2 % 2


def bit_b(i):
    return i // 2


def device_at(device):
    dp, t = device // 4, device % 4
    return dp // 32, dp // 8 % 4, dp // 2 % 4, dp % 2, t


def move(array, target):
    pairs = []
    for device in range(256):
        zl, x, y, c, t = target(*device_at(device))
        pairs.append((device, (((zl * 4 + x) * 4 + y) * 2 + c) * 4 + t))
    return lax.ppermute(array, AXES, pairs)


def to_other_core(array):
    return move(array, lambda zl, x, y, c, t: (zl, x, y, 1 - c, t))


def in_square(array, flip, of_places):
    def target(zl, x, y, c, t):
        x2, y2 = (x ^ 1, y ^ 1) if (c == 0) == of_places else (3 - x, 3 - y)
        return zl, x2 if flip & 2 else x, y2 if flip & 1 else y, c, t

    return move(array, target)


def to_slab(array, step):
    return move(array, lambda zl, x, y, c, t: (zl, x, y, c, t ^ 1 if c == step else 3 - t))


def to_slab_and_neighbour(array):
    def target(zl, x, y, c, t):
        return 1 - zl, x, y, c, t ^ 1 if c == 1 else 3 - t

    return move(array, target)


def to_z_neighbour(array):
    return move(array, lambda zl, x, y, c, t: (1 - zl, x, y, c, t))


def here(dev):
    dp = dev[0] // 4
    core, x, y = dp % 2, dp // 8 % 4, dp // 2 % 4
    a, b = 2 * bit_a(x) + bit_a(y), 2 * bit_b(x) + bit_b(y)
    return core, jnp.where(core == 0, a, b), jnp.where(core == 0, b, a)


def pack_kernel(dev, act, *refs):
    outs, sem = refs[:-1], refs[-1]
    core, mine, across = here(dev)
    t = dev[0] % 4
    copies = []
    for half in range(2):
        *own, sent = outs[(RING + 1) * half : (RING + 1) * (half + 1)]
        for side in (1, 0):
            first = jnp.where(core == side, t ^ 1, 3 - t)
            second = jnp.where(core == side, 3 - t, t ^ 1)
            for flip in range(RING):
                place = (across if side else mine) ^ flip
                for rank, slab in enumerate((t, second) if half else (first, t ^ 2)):
                    start = pl.multiple_of((2 * slab + place % 2) * BLOCK, TILE)
                    copies.append(
                        pltpu.make_async_copy(
                            act.at[core ^ side, place // 2, :, pl.ds(start, BLOCK)],
                            (sent.at[flip] if side else own[flip]).at[rank],
                            sem.at[len(copies)],
                        )
                    )
                    copies[-1].start()
    for copy in copies:
        copy.wait()


def gram_kernel(dev, *refs):
    ins, outs, tri = refs[: 2 * RING], refs[2 * RING : 3 * RING], refs[3 * RING]
    ins = [*ins[:-1], ins[-1].at[0]]
    across = here(dev)[2]
    for slab in range(2):

        def product(low, high):
            return lax.dot_general(
                jnp.concatenate([ref[slab, :, low:high] for ref in ins]),
                jnp.concatenate([ref[slab, :, low:] for ref in ins]),
                (((0,), (0,)), ((), ())),
                preferred_element_type=jnp.float32,
            )

        top = product(0, 256)
        tri[0:128, :] = top[0:128]
        tri[128:256, 0:512] = top[128:256, 128:]
        middle = product(256, 512)
        tri[256:384, 0:384] = middle[0:128]
        tri[256:384, 384:640] = middle[128:256, 128:]
        tri[128:256, 512:640] = product(512, 640)
        for flip in range(RING):
            start = pl.multiple_of((across ^ flip) * CHUNK, 32)
            outs[flip][slab] = tri[pl.ds(start, CHUNK), :].astype(jnp.bfloat16)


def newton_kernel(tokens_all, dev, newton_steps, *refs):
    ins, (out, total, mixed, gap, mixed_half, gap_half) = refs[:RING], refs[RING:]
    t = dev[0] % 4
    core, place, across = here(dev)
    for flip in range(RING):
        start = pl.multiple_of((across ^ flip) * CHUNK, 32)
        total[pl.ds(start, CHUNK), :] = ins[3 - flip][...]
    steps = newton_steps[core, place // 2, 2 * t + place % 2]
    eye = (
        lax.broadcasted_iota(jnp.int32, (BLOCK, BLOCK), 0)
        == lax.broadcasted_iota(jnp.int32, (BLOCK, BLOCK), 1)
    ).astype(jnp.float32)
    squares = jnp.zeros((TILE, TILE), jnp.float32)
    for i, (row, col) in enumerate(PANELS):
        low = TILE * i
        panel = total[row : row + TILE, col : col + BLOCK - low]
        for j in range(i, 5):
            tile = panel[:, TILE * (j - i) : TILE * (j - i + 1)].astype(jnp.float32)
            tile = tile * (1.0 / tokens_all)
            if i == j:
                tile = tile + DAMPING * eye[:TILE, :TILE]
            mixed[low : low + TILE, TILE * j : TILE * (j + 1)] = tile
            squares = squares + (1.0 if i == j else 2.0) * tile * tile
            if (i, j) in ((0, 1), (2, 3)):
                mixed[TILE * j : TILE * (j + 1), low : low + TILE] = tile.T
    norm_scale = jnp.sqrt(jnp.sum(squares))
    scale = 1.0 / norm_scale

    def dot(a, b):
        return jnp.dot(a, b, preferred_element_type=jnp.float32)

    bands = (slice(0, 256), slice(256, 512), slice(512, 640))

    def keep(whole, band, value):
        value = value.astype(jnp.bfloat16)
        whole[band, band.start :] = value
        if band.stop < BLOCK:
            whole[band.stop :, band] = value[:, band.stop - band.start :].T

    for band in bands:
        start = mixed[band, band.start :] * scale
        gap[band, band.start :] = start
        keep(mixed_half.at[0], band, start)
        keep(gap_half.at[1], band, start)
    for band in bands:
        right = slice(band.start, BLOCK)
        value = 2.0 * gap[band, right] - dot(mixed_half[0, band, :], mixed_half[0, :, right])
        mixed[band, right] = value
        keep(mixed_half.at[1], band, value)
    for turn in range(1, 3):
        now = turn % 2
        for band in bands:
            right = slice(band.start, BLOCK)
            old, old_gap, operand = mixed[band, right], gap[band, right], mixed_half[now, :, right]
            new = 2.0 * old - dot(mixed_half[now, band, :], operand)
            mixed[band, right] = new
            keep(mixed_half.at[1 - now], band, new)
            new_gap = 2.0 * old_gap + 2.0**turn * old - dot(gap_half[now, band, :], operand)
            new_gap = jnp.where(turn < steps, new_gap, old_gap)
            gap[band, right] = new_gap
            keep(gap_half.at[1 - now], band, new_gap)
    reach = jnp.where(steps <= 1, 2.0, jnp.where(steps == 2, 4.0, jnp.where(steps == 3, 8.0, 16.0)))
    for band in bands:
        begin = band.start
        old_gap = gap[band, begin:]
        new_gap = 2.0 * old_gap + 8.0 * mixed[band, begin:]
        new_gap = new_gap - dot(gap_half[1, band, :], mixed_half[1, :, begin:])
        value = reach * eye[band, begin:] - jnp.where(3 < steps, new_gap, old_gap)
        value = (value * scale).astype(jnp.bfloat16)
        for i in range(begin // TILE, band.stop // TILE):
            row, col = PANELS[i]
            low = TILE * i
            out[row : row + TILE, col : col + BLOCK - low] = value[
                low - begin : low - begin + TILE, low - begin :
            ]


def apply_kernel(side, dev, *refs):
    ins, grads, outs = refs[:RING], refs[RING : RING + 2], refs[-6:-4]
    outs_here, whole, sem = refs[-4:-2], refs[-2], refs[-1]
    core, mine, across = here(dev)
    layer = core ^ side
    mine = across if side else mine
    stores = []

    def unfold(block, place):
        for i, (row, col) in enumerate(PANELS):
            low = TILE * i
            panel = block[row : row + TILE, col : col + BLOCK - low]
            whole[place, low : low + TILE, low:] = panel
            if i % 2 == 0 and i < 4:
                whole[place, low + TILE : low + 2 * TILE, low : low + TILE] = panel[
                    :, TILE : 2 * TILE
                ].T

    def dot(a, b):
        return jnp.dot(a, b, preferred_element_type=jnp.float32)

    def dot_transposed(a, b):
        return lax.dot_general(a, b, (((1,), (1,)), ((), ())), preferred_element_type=jnp.float32)

    for flip in range(RING):
        unfold(ins[flip], mine ^ flip)
    for place in range(RING):
        kind, j = place // 2, place % 2
        at = j * BLOCK

        def columns(start, stop):
            return grads[kind][layer, :, at + start : at + stop]

        part_0, part_1 = columns(0, 256), columns(256, 512)
        part_2, part_12 = columns(512, 640), columns(256, 640)
        top = dot(part_0, whole[place, 0:256, :])
        middle = dot(part_1, whole[place, 256:512, 256:])
        low = dot(part_2, whole[place, 512:640, 512:])
        left = top[:, 0:256] + dot_transposed(part_12, whole[place, 0:256, 256:])
        centre = (
            top[:, 256:512]
            + middle[:, 0:256]
            + dot_transposed(part_2, whole[place, 256:512, 512:])
        )
        right = top[:, 512:] + middle[:, 256:] + low
        outs_here[kind][:, at : at + 256] = left.astype(jnp.bfloat16)
        outs_here[kind][:, at + 256 : at + 512] = centre.astype(jnp.bfloat16)
        outs_here[kind][:, at + 512 : at + 640] = right.astype(jnp.bfloat16)
        done = pl.ds(at, BLOCK)
        stores.append(
            pltpu.make_async_copy(
                outs_here[kind].at[:, done], outs[kind].at[layer, :, done], sem.at[place]
            )
        )
        stores[-1].start()
    for store in stores:
        store.wait()


def local(activations, grad_qkv, grad_up, newton_steps):
    half = jnp.bfloat16
    dev = (lax.axis_index("dp") * 4 + lax.axis_index("tensor")).astype(jnp.int32).reshape(1)
    rows = activations.shape[2]
    tokens_all = rows * 256

    def shape(*dims):
        return jax.ShapeDtypeStruct(dims, half)

    def wide(array):
        return array.astype(jnp.float32)

    def over_square(parts, of_places):
        moved = {flip: in_square(parts[flip], flip, of_places) for flip in (3, 2, 1)}
        return [parts[0]] + [moved[flip] for flip in (1, 2, 3)]

    part = (2, rows, BLOCK)
    packed = pl.pallas_call(
        pack_kernel,
        out_shape=([shape(*part)] * RING + [shape(RING, *part)]) * 2,
        in_specs=[SMEM, ANY],
        out_specs=[ANY] * (2 * RING + 2),
        scratch_shapes=[pltpu.SemaphoreType.DMA((4 * RING * 2,))],
        compiler_params=pltpu.CompilerParams(vmem_limit_bytes=48 * 1024 * 1024),
        name="pack",
    )(dev, activations)

    def factors(own, sent):
        received = to_other_core(sent)
        own = over_square(own, True)
        others = [in_square(received[flip], flip, True) for flip in (3, 2, 1)]
        chunks = pl.pallas_call(
            gram_kernel,
            out_shape=[shape(2, CHUNK, BLOCK)] * RING,
            in_specs=[SMEM] + [VMEM] * (2 * RING),
            out_specs=[VMEM] * RING,
            scratch_shapes=[pltpu.VMEM((PACK, BLOCK), jnp.float32)],
            compiler_params=PARAMS,
            name="gram",
        )(dev, *own[::-1], *others, received)
        chunks = over_square(chunks, False)
        return sum(wide(chunk) for chunk in chunks[::-1])

    leaving = to_slab(factors(packed[:RING], packed[RING]).astype(half), 0)
    sums = factors(packed[RING + 1 : -1], packed[-1]) + wide(leaving)
    stays, leaves = sums[0].astype(half), sums[1].astype(half)
    arrived = [to_slab_and_neighbour(leaves), to_slab(leaves, 1), to_z_neighbour(stays)]
    sums = sums[0] + sum(wide(array) for array in arrived)
    members = over_square([sums.astype(half)] * RING, False)

    inverse = pl.pallas_call(
        functools.partial(newton_kernel, tokens_all),
        out_shape=shape(PACK, BLOCK),
        in_specs=[SMEM, SMEM] + [VMEM] * RING,
        out_specs=VMEM,
        scratch_shapes=[
            pltpu.VMEM((PACK, BLOCK), half),
            pltpu.VMEM((BLOCK, BLOCK), jnp.float32),
            pltpu.VMEM((BLOCK, BLOCK), jnp.float32),
            pltpu.VMEM((2, BLOCK, BLOCK), half),
            pltpu.VMEM((2, BLOCK, BLOCK), half),
        ],
        compiler_params=PARAMS,
        name="newton",
    )(dev, newton_steps, *members[::-1])
    mine = over_square([inverse] * RING, True)
    others = [to_other_core(block) for block in mine]

    def apply(side, blocks, before):
        kinds = (grad_qkv.shape, grad_up.shape)
        buffers = [pltpu.VMEM(dims[1:], half) for dims in kinds]
        return pl.pallas_call(
            functools.partial(apply_kernel, side),
            out_shape=[shape(*dims) for dims in kinds],
            in_specs=[SMEM] + [VMEM] * (RING + 2) + [ANY] * len(before),
            out_specs=[ANY] * 2,
            input_output_aliases={7: 0, 8: 1} if before else {},
            scratch_shapes=buffers
            + [
                pltpu.VMEM((RING, BLOCK, BLOCK), half),
                pltpu.SemaphoreType.DMA((4,)),
            ],
            compiler_params=PARAMS,
            name="apply",
        )(dev, *blocks, grad_qkv, grad_up, *before)

    return tuple(apply(1, others, apply(0, mine, ())))


def solution(mesh):
    placed = (
        P(None, None, ("dp", "tensor"), None),
        P(None, "dp", "tensor"),
        P(None, "dp", "tensor"),
        P(),
    )
    return jax.shard_map(
        local,
        mesh=mesh,
        in_specs=placed,
        out_specs=(P(None, "dp", "tensor"), P(None, "dp", "tensor")),
        check_vma=False,
    )
```
